256 devices in a mesh: in: 8 (over z), out: 4 (over y_hi, core), dep: 8 (over x, y_lo).
Axes of the slice: x: 4, y: 4 (y_hi: 2, y_lo: 2; y = y_hi * 2 + y_lo), z: 8, core: 2. Of those that a mesh axis runs over, the one named last changes fastest.
Arguments:
- tokens: bfloat16 [8, 512, 3072], P('dep', 'in', 'out'), may hold values from -48 to 48
- norm_gain: float32 [3072], P('out'), may hold values from 0.1 to 1.9
- qkv_weight: bfloat16 [3072, 3, 3072], P(('out', 'dep'), None, 'in'), may hold values from -0.109375 to 0.109375
- head_gain: float32 [2, 128], replicated, may hold values from 1 to 5, as said below
- out_weight: bfloat16 [3072, 3072], P(('in', 'dep'), 'out'), may hold values from -0.109375 to 0.109375
- up_weight: bfloat16 [3072, 12288], P(('out', 'dep'), 'in'), may hold values from -0.109375 to 0.109375
- down_weight: bfloat16 [12288, 3072], P(('in', 'dep'), 'out'), may hold values from -0.0546875 to 0.0546875
- upstream: bfloat16 [8, 512, 3072], P('dep', 'in', 'out'), may hold values from -6 to 6
Outputs:
- layer_out: bfloat16 [8, 512, 3072], P('dep', 'in', 'out')
- token_grad: bfloat16 [8, 512, 3072], P('dep', 'in', 'out')
- norm_gain_grad: float32 [3072], P('out')
- head_gain_grad: float32 [2, 128], replicated
- qkv_weight_grad: float32 [3072, 3, 3072], P(('out', 'dep'), None, 'in')
- out_weight_grad: float32 [3072, 3072], P(('in', 'dep'), 'out')
- up_weight_grad: float32 [3072, 12288], P(('out', 'dep'), 'in')
- down_weight_grad: float32 [12288, 3072], P(('in', 'dep'), 'out')
The draws below stay inside these ranges and needn't reach their ends.
Inputs may be any that keep to these rules, and one draw needn't show every extreme that they name: `head_gain`: every entry is positive.
All inputs are finite; a program needn't handle non-finite values.
Results may differ from the reference program's by a relative error of at most 0.02.
The reference program's roundings to bfloat16 on the way (of `hidden_in`, `weights_low`, `attended_low`, `activated_low`, `attended_grad`, `before_grad`, `score_grad` and `qkv_grad`) count: a program that leaves them out, or rounds other values in their place, can miss the bound.
Values may be sent and summed in bfloat16 or wider, within the bound.
A program may use at most 128 MiB of HBM per device.

```python
import math
import jax
import jax.numpy as jnp
from jax import lax

D = 3072
HEADS = 24
HEAD_DIM = 128
FF = 12288
ATTN = 3072
SEQ = 512
CLIPS = 8


def draw_tokens(key, part):
    key = jax.random.fold_in(key, 11)
    base_key, column_key = jax.random.split(key, 2)
    position = jnp.arange(D, dtype=jnp.float32) / D
    rising = jnp.exp(position * math.log(3.0))
    factor = jax.random.uniform(column_key, (1, 1, D), jnp.float32, 0.5, 2.0)
    values = jnp.clip(jax.random.normal(base_key, (CLIPS, SEQ, D), jnp.float32), -4.0, 4.0)
    return (values * rising * factor).astype(jnp.bfloat16)


def draw_head_gain(key, part):
    key = jax.random.fold_in(key, 23)
    values = jax.random.uniform(key, (2, HEAD_DIM), jnp.float32, 1.0, 1.6)
    return values


def steps_of(stream_key, dims, cuts, low, high):
    def one(dim, shards_of):
        heights = jax.random.uniform(jax.random.fold_in(jax.random.fold_in(stream_key, 6), dim), (shards_of,), jnp.float32, low / len(cuts), high / len(cuts))
        return jnp.repeat(jnp.exp(heights), dims[dim] // shards_of).reshape((-1,) + (1,) * (len(dims) - dim - 1))

    loudness = one(*cuts[0])
    for cut in cuts[1:]:
        loudness = loudness * one(*cut)
    return loudness


def noise(rng, extent, width, bound, pieces=(), kind=jnp.bfloat16):
    drawn = jax.random.normal(rng, extent, jnp.float32) * width
    if len(pieces) > 0:
        drawn = steps_of(rng, extent, pieces, -0.22, 0.18) * drawn
    return jnp.clip(drawn, min=-bound, max=bound).astype(kind)


def setup_inputs(seed: int = 0) -> dict:
    streams_of = jax.random.split(jax.random.key(seed), 9)
    tokens = draw_tokens(jax.random.fold_in(streams_of[8], 71), 0)
    norm_gain = jnp.clip(1.0 + 0.18 * jax.random.normal(streams_of[1], (D,), jnp.float32), 0.1, 1.9)
    qkv_weight = noise(streams_of[2], (D, 3, ATTN), D ** -0.5, 0.109375, ((0, 32), (2, 8)))
    head_gain = draw_head_gain(jax.random.fold_in(streams_of[8], 71), 0)
    out_weight = noise(streams_of[4], (ATTN, D), ATTN ** -0.5, 0.109375, ((0, 64), (1, 4)))
    up_weight = noise(streams_of[5], (D, FF), D ** -0.5, 0.109375, ((0, 32), (1, 8)))
    down_weight = noise(streams_of[6], (FF, D), FF ** -0.5, 0.0546875, ((0, 64), (1, 4)))
    upstream = noise(streams_of[7], (CLIPS, SEQ, D), 1.0, 6.0, ((0, 8), (1, 8), (2, 4)))
    return dict(tokens=tokens, norm_gain=norm_gain, qkv_weight=qkv_weight, head_gain=head_gain, out_weight=out_weight, up_weight=up_weight, down_weight=down_weight, upstream=upstream)


EPSILON = 1e-06
ROOT_HALF = 1.0 / math.sqrt(2.0)
ROOT_TWO_PI = math.sqrt(2.0 * math.pi)

def normalize(values):
    average = lax.optimization_barrier(jnp.mean(values, axis=-1, keepdims=True))
    spread = lax.optimization_barrier(jnp.mean(values * values, axis=-1, keepdims=True)) - average * average
    inverse = lax.rsqrt(spread + EPSILON)
    return ((values - average) * inverse, inverse)

def normalize_back(incoming, normed, inverse):
    first = lax.optimization_barrier(jnp.mean(incoming, axis=-1, keepdims=True))
    second = lax.optimization_barrier(jnp.mean(incoming * normed, axis=-1, keepdims=True))
    return inverse * (incoming - first - normed * second)

def gelu_pair(values):
    below = 0.5 * (1.0 + jax.scipy.special.erf(values * ROOT_HALF))
    slope = below + values * jnp.exp(-0.5 * values * values) / ROOT_TWO_PI
    return (values * below, slope)

def per_clip(values):
    return values.reshape((CLIPS, SEQ) + values.shape[1:])

def grouped_product(left, right):

    def step(carry, pair):
        product = jnp.dot(pair[0].T, pair[1], preferred_element_type=jnp.float32)
        rounded = lax.optimization_barrier(product.astype(jnp.bfloat16))
        return (carry + rounded.astype(jnp.float32), None)
    initial = jnp.zeros((left.shape[1], right.shape[1]), jnp.float32)
    summed, _ = lax.scan(step, initial, (per_clip(left), per_clip(right)))
    return summed

def to_heads(values):
    shaped = values.reshape(CLIPS, SEQ, HEADS, HEAD_DIM)
    return jnp.transpose(shaped, (0, 2, 1, 3)).reshape(CLIPS * HEADS, SEQ, HEAD_DIM)

def from_heads(values):
    shaped = values.reshape(CLIPS, HEADS, SEQ, HEAD_DIM)
    return jnp.transpose(shaped, (0, 2, 1, 3)).reshape(CLIPS * SEQ, HEADS, HEAD_DIM)

def head_pass(operands):
    query, key_rows, value_rows, incoming = operands
    scale = HEAD_DIM ** (-0.5)
    scores = jnp.dot(query, key_rows.T, preferred_element_type=jnp.float32) * scale
    highest = lax.optimization_barrier(jnp.max(scores, axis=-1, keepdims=True))
    raised = jnp.exp(scores - highest)
    weights = raised / lax.optimization_barrier(jnp.sum(raised, axis=-1, keepdims=True))
    weights_low = weights.astype(jnp.bfloat16)
    attended = jnp.dot(weights_low, value_rows, preferred_element_type=jnp.float32)
    slopes = jnp.dot(incoming, value_rows.T, preferred_element_type=jnp.float32)
    centre = lax.optimization_barrier(jnp.sum(weights * slopes, axis=-1, keepdims=True))
    score_grad = (weights * (slopes - centre)).astype(jnp.bfloat16)
    query_grad = jnp.dot(score_grad, key_rows, preferred_element_type=jnp.float32) * scale
    key_grad = jnp.dot(score_grad.T, query, preferred_element_type=jnp.float32) * scale
    value_grad = jnp.dot(weights_low.T, incoming, preferred_element_type=jnp.float32)
    return (attended, query_grad, key_grad, value_grad)

def reference(tokens, norm_gain, qkv_weight, head_gain, out_weight, up_weight, down_weight, upstream):
    total = CLIPS * SEQ
    flat_tokens = tokens.reshape(total, D)
    flat_upstream = upstream.reshape(total, D)
    wide = flat_tokens.astype(jnp.float32)
    normed, inverse = normalize(wide)
    hidden_in = (normed * norm_gain).astype(jnp.bfloat16)
    qkv_flat = qkv_weight.reshape(D, 3 * ATTN)
    projected = jnp.dot(hidden_in, qkv_flat, preferred_element_type=jnp.float32).reshape(total, 3, HEADS, HEAD_DIM)
    before = jnp.dot(hidden_in, up_weight, preferred_element_type=jnp.float32)
    query_hat, query_inverse = normalize(projected[:, 0])
    key_hat, key_inverse = normalize(projected[:, 1])
    query_low = (query_hat * head_gain[0]).astype(jnp.bfloat16)
    key_low = (key_hat * head_gain[1]).astype(jnp.bfloat16)
    value_low = projected[:, 2].astype(jnp.bfloat16)
    attended_grad = jnp.dot(flat_upstream, out_weight.T, preferred_element_type=jnp.float32)
    attended_grad = attended_grad.astype(jnp.bfloat16).reshape(total, HEADS, HEAD_DIM)
    head_major = tuple((to_heads(member) for member in (query_low, key_low, value_low, attended_grad)))
    attended, query_grad, key_grad, value_grad = lax.map(head_pass, head_major)
    attended_low = from_heads(attended).reshape(total, ATTN).astype(jnp.bfloat16)
    query_grad = from_heads(query_grad)
    key_grad = from_heads(key_grad)
    value_grad = from_heads(value_grad)
    activated, slope = gelu_pair(before)
    activated_low = activated.astype(jnp.bfloat16)
    mixed = wide + jnp.dot(attended_low, out_weight, preferred_element_type=jnp.float32)
    mixed = mixed + jnp.dot(activated_low, down_weight, preferred_element_type=jnp.float32)
    layer_out = mixed.astype(jnp.bfloat16).reshape(CLIPS, SEQ, D)
    inner_grad = jnp.dot(flat_upstream, down_weight.T, preferred_element_type=jnp.float32)
    before_grad = (inner_grad * slope).astype(jnp.bfloat16)
    query_back = normalize_back(query_grad * head_gain[0], query_hat, query_inverse)
    key_back = normalize_back(key_grad * head_gain[1], key_hat, key_inverse)
    head_gain_grad = jnp.stack([lax.optimization_barrier(jnp.sum(query_grad * query_hat, axis=(0, 1))), lax.optimization_barrier(jnp.sum(key_grad * key_hat, axis=(0, 1)))])
    qkv_grad = jnp.stack([query_back, key_back, value_grad], axis=1).reshape(total, 3 * ATTN).astype(jnp.bfloat16)
    input_grad = jnp.dot(qkv_grad, qkv_flat.T, preferred_element_type=jnp.float32)
    input_grad = input_grad + jnp.dot(before_grad, up_weight.T, preferred_element_type=jnp.float32)
    norm_gain_grad = lax.optimization_barrier(jnp.sum(input_grad * normed, axis=0))
    scaled = input_grad * norm_gain
    token_grad = (flat_upstream.astype(jnp.float32) + normalize_back(scaled, normed, inverse)).astype(jnp.bfloat16)
    token_grad = token_grad.reshape(CLIPS, SEQ, D)
    qkv_weight_grad = grouped_product(hidden_in, qkv_grad).reshape(D, 3, ATTN)
    up_weight_grad = grouped_product(hidden_in, before_grad)
    out_weight_grad = grouped_product(attended_low, flat_upstream)
    down_weight_grad = grouped_product(activated_low, flat_upstream)
    return (layer_out, token_grad, norm_gain_grad, head_gain_grad, qkv_weight_grad, out_weight_grad, up_weight_grad, down_weight_grad)
```

```python
import math

import jax
import jax.numpy as jnp
from jax import lax
from jax.experimental import pallas as pl
from jax.experimental.pallas import tpu as pltpu
from jax.sharding import PartitionSpec as P

MESH = pl.DeviceIdType.MESH
EPSILON = 1e-06
ROOT_HALF = 1.0 / math.sqrt(2.0)
ROOT_TWO_PI = math.sqrt(2.0 * math.pi)
SCALE = 128.0 ** (-0.5)
F32 = jnp.float32
BF16 = jnp.bfloat16
VMEM = pltpu.VMEM

TILES = (384, 384, 512, 512)
COLS = (1152, 384, 1536, 1536)
SHARD = ((96, 1152), (48, 768), (96, 1536), (192, 768))
SPLIT = (48, 32, 48, 96)
RING = (1, 7, 2, 6, 3, 5, 4)


def remote(src, dst, send, recv, device):
    return pltpu.make_async_remote_copy(
        src_ref=src, dst_ref=dst, send_sem=send, recv_sem=recv, device_id=device, device_id_type=MESH
    )


class Place:
    def __init__(self):
        self.i = lax.axis_index("in")
        self.o = lax.axis_index("out")
        self.d = lax.axis_index("dep")
        d = self.d
        x, y = d // 2, d % 2
        right, left, far = (x + 1) % 4, (x + 3) % 4, (x + 2) % 4
        self.me = d
        self.r, self.l, self.f = right * 2 + y, left * 2 + y, far * 2 + y
        self.p = x * 2 + 1 - y
        self.rp, self.lp, self.fp = right * 2 + 1 - y, left * 2 + 1 - y, far * 2 + 1 - y
        self.h, self.c = self.o // 2, self.o % 2
        self.mate = self.h * 2 + 1 - self.c
        self.cross = (1 - self.h) * 2 + self.c
        self.mate_at = {"out": self.mate}
        self.cross_at = {"out": self.cross, "dep": self.p}
        self.diag_at = {"out": (1 - self.h) * 2 + 1 - self.c, "dep": self.p}
        self.diag = (1 - self.h) * 2 + 1 - self.c
        self.table = (
            (self.r, self.l, self.me, self.l, "all"),
            (self.l, self.r, self.me, self.r, "all"),
            (self.p, self.p, self.me, self.p, "all"),
            (self.r, self.l, self.l, self.f, "low"),
            (self.l, self.r, self.r, self.f, "high"),
            (self.r, self.l, self.p, self.lp, "all"),
            (self.l, self.r, self.p, self.rp, "all"),
            (self.p, self.p, self.f, self.fp, "all"),
        )


def rows_of(slot, rows, split, part):
    start = slot * rows
    if part == "all":
        return pl.ds(pl.multiple_of(start, 16), rows)
    if part == "low":
        return pl.ds(pl.multiple_of(start, 16), split)
    return pl.ds(pl.multiple_of(start + split, 16), rows - split)


def greet(place):
    barrier = pltpu.get_barrier_semaphore()
    for k in range(1, 8):
        pl.semaphore_signal(barrier, inc=1, device_id={"in": (place.i + k) % 8}, device_id_type=MESH)
        pl.semaphore_signal(barrier, inc=1, device_id={"dep": (place.d + k) % 8}, device_id_type=MESH)
    for peer in (place.mate_at, place.cross_at, place.diag_at):
        pl.semaphore_signal(barrier, inc=1, device_id=peer, device_id_type=MESH)
    pl.semaphore_wait(barrier, 17)


def dot(a, b):
    return lax.dot_general(a, b, (((1,), (0,)), ((), ())), preferred_element_type=F32)


def dot_nt(a, b):
    return lax.dot_general(a, b, (((1,), (1,)), ((), ())), preferred_element_type=F32)


def dot_tn(a, b):
    return lax.dot_general(a, b, (((0,), (0,)), ((), ())), preferred_element_type=F32)


def normalize(values):
    average = jnp.mean(values, axis=-1, keepdims=True)
    spread = jnp.mean(values * values, axis=-1, keepdims=True) - average * average
    inverse = lax.rsqrt(spread + EPSILON)
    return ((values - average) * inverse, inverse)


def normalize_back(incoming, normed, inverse):
    first = jnp.mean(incoming, axis=-1, keepdims=True)
    second = jnp.mean(incoming * normed, axis=-1, keepdims=True)
    return inverse * (incoming - first - normed * second)


def layer_kernel(
    tokens, gain, head_gain, upstream, wq, wo, wu, wd,
    layer_out, token_grad, gain_grad, head_grad, dq, do, du, dd,
    gq, go, gu, gd, hid, grad, normed, inverse, fq, fo, fu, fd,
    stat_out, stat_in, own0, own1, own2, own3, lo0, lo1, lo2, lo3, in0, in1, in2, in3,
    xs_f, xs_q, xs_o, xs_u, xs_d, xr_f, xr_q, xr_o, xr_u, xr_d,
    kv, att, act, bg, qg, qlow, alow, hats, invs, kvpart, kvin, kvs, kvr,
    tok, ups, hid_t, lo_buf, lo_in, tg_buf, tg_in,
    pq, po, pu, pd, rq, ro, ru, rd, zsend0, zsend1, zin0, zin1, zown0, zown1,
    tot_out, tot_in, vz_out, vz_in, vd_out, vd_in, hz_out, hz_in, hd_out, hd_in, ho_out, ho_in,
    gs, gr, gl, zs, zr, ss, sr, ms, mr, cs, cr, bs, br, ks, kr, ws, wr, vs, vr, es, er,
):
    place = Place()
    shards = (wq, wo, wu, wd)
    gathered = (gq, go, gu, gd)
    own, lo, arrived, final = (own0, own1, own2, own3), (lo0, lo1, lo2, lo3), (in0, in1, in2, in3), (fq, fo, fu, fd)
    partial, returned, result = (pq, po, pu, pd), (rq, ro, ru, rd), (dq, do, du, dd)
    greet(place)
    pending = []

    def start(copy):
        copy.start()
        pending.append(copy)

    def local(src, dst, sem):
        copy = pltpu.make_async_copy(src, dst, sem)
        copy.start()
        return copy

    def slots(a, ref, rows):
        return ref.at[:, rows] if a == 0 else ref.at[rows]

    def gather_copy(a, k, receive=False):
        rows, _ = SHARD[a]
        target, _, mine, theirs, part = place.table[k]
        ref = slots(a, gathered[a], rows_of(theirs if receive else mine, rows, SPLIT[a], part))
        source = ref if receive or k > 2 else shards[a]
        return remote(source, ref, gs.at[a, k], gr.at[a, k], {"dep": target})

    def g_send(a, *kinds):
        for k in kinds:
            start(gather_copy(a, k))

    def g_wait(a, *kinds):
        for k in kinds:
            gather_copy(a, k, True).wait_recv()

    own_copies = [None] * 4

    def stage1(a):
        g_send(a, 0, 1, 2)
        rows, _ = SHARD[a]
        own_copies[a] = local(shards[a], slots(a, gathered[a], rows_of(place.me, rows, 0, "all")), gl.at[a])

    def stage2(a):
        g_wait(a, 0)
        g_send(a, 3)
        g_wait(a, 1)
        g_send(a, 4)
        g_wait(a, 2)
        g_send(a, 5, 6)

    def stage3(a):
        g_wait(a, 3, 4)
        g_send(a, 7)

    def stage4(a):
        g_wait(a, 5, 6, 7)
        own_copies[a].wait()

    def z_slot(ref, index):
        return ref.at[pl.ds(pl.multiple_of(index * 64, 64), 64)]

    def z_ring_copy(which, kind, ref, receive=False):
        turn = kind % 4
        if kind < 4:
            target, slot = (place.i + 1) % 8, (place.i + (7 if receive else 8) - turn) % 8
        else:
            target, slot = (place.i + 7) % 8, (place.i + (1 if receive else 0) + turn) % 8
        first = 32 if kind == 7 else 0
        at = ref.at[pl.ds(pl.multiple_of(slot * 64 + first, 32), 32 if turn == 3 else 64)]
        return remote(at, at, zs.at[which, kind], zr.at[which, kind], {"in": target})

    def z_round(which, ref, turn):
        for way in (0, 4):
            if turn > 0:
                z_ring_copy(which, way + turn - 1, ref, True).wait_recv()
            start(z_ring_copy(which, way + turn, ref))

    def z_done(which, ref):
        for way in (0, 4):
            z_ring_copy(which, way + 3, ref, True).wait_recv()

    def zsum_copy(which, k, send, recv):
        to = (place.i + k) % 8
        return remote(z_slot(send, to), recv.at[k - 1], zs.at[which, k - 1], zr.at[which, k - 1], {"in": to})

    def zsum_send(which, send, recv):
        for k in RING:
            start(zsum_copy(which, k, send, recv))

    def zsum_total(which, send, recv, mine):
        total = mine[...]
        for k in RING:
            zsum_copy(which, k, send, recv).wait_recv()
            total = total + recv[k - 1].astype(F32)
        return total

    def fan_copy(axis, index, size, k, send, recv, sem_s, sem_r):
        if axis == "out":
            peer = (place.mate_at, place.cross_at, place.diag_at)[k - 1]
        else:
            peer = {axis: (index + k) % size}
        return remote(send, recv.at[k - 1], sem_s.at[k - 1], sem_r.at[k - 1], peer)

    def fan_send(axis, index, size, send, recv, sem_s, sem_r):
        for k in range(1, size):
            start(fan_copy(axis, index, size, k, send, recv, sem_s, sem_r))

    def fan_total(axis, index, size, send, recv, sem_s, sem_r):
        total = send[...]
        for k in range(1, size):
            fan_copy(axis, index, size, k, send, recv, sem_s, sem_r).wait_recv()
            total = total + recv[k - 1]
        return total

    def out_rows(ref, index):
        return ref.at[pl.ds(pl.multiple_of(index * 128, 128), 128)]

    def out_copy(which, k, ref, receive=False):
        sent = (place.o, place.o, place.cross)[k]
        got = (place.mate, place.cross, place.diag)[k]
        target = (place.mate_at, place.cross_at, place.mate_at)[k]
        rows = out_rows(ref, got if receive else sent)
        return remote(rows, rows, bs.at[which, k], br.at[which, k], target)

    def out_send(which, ref):
        start(out_copy(which, 1, ref))
        start(out_copy(which, 0, ref))

    def out_relay(which, ref):
        out_copy(which, 1, ref, True).wait_recv()
        start(out_copy(which, 2, ref))

    def out_wait(which, ref):
        out_copy(which, 0, ref, True).wait_recv()
        out_copy(which, 2, ref, True).wait_recv()

    def swap_copy(k, source, landing):
        return remote(source, landing, es.at[k], er.at[k], {"dep": place.p})

    def swap_start(k, source, landing, result):
        @pl.when(place.h == 1)
        def _():
            swap_copy(k, source, landing).start()

        @pl.when(place.h == 0)
        def _():
            result[...] = source[...]

    def swap_end(k, source, landing, result):
        @pl.when(place.h == 1)
        def _():
            swap_copy(k, source, landing).wait()
            if result is not landing:
                result[...] = landing[...]

    swap_start(0, tokens, tok, tok)
    swap_start(1, upstream, ups, ups)
    stage1(0)
    stage1(1)
    swap_end(0, tokens, tok, tok)

    wide = tok[...].astype(F32)
    lane = lax.broadcasted_iota(jnp.int32, (64, 128), 1)
    total = jnp.sum(wide, axis=1, keepdims=True)
    square = jnp.sum(wide * wide, axis=1, keepdims=True)
    stat_out[...] = jnp.where(lane < 64, total, square)
    fan_send("out", place.o, 4, stat_out, stat_in, ss.at[0], sr.at[0])
    swap_end(1, upstream, ups, ups)
    z_slot(grad, place.i)[...] = ups[...]
    stats = fan_total("out", place.o, 4, stat_out, stat_in, ss.at[0], sr.at[0])
    average = stats[:, :1] * (1.0 / 3072.0)
    spread = stats[:, 64:65] * (1.0 / 3072.0) - average * average
    inv = lax.rsqrt(spread + EPSILON)
    norm = (wide - average) * inv
    normed[...] = norm
    inverse[...] = jnp.broadcast_to(inv, (64, 128))
    z_slot(hid, place.i)[...] = (norm * gain[...]).astype(BF16)
    z_round(0, hid, 0)
    z_round(1, grad, 0)
    stage2(0)
    z_round(0, hid, 1)
    stage1(2)
    stage2(1)
    z_round(0, hid, 2)
    stage3(0)
    z_round(1, grad, 1)
    z_round(0, hid, 3)
    stage3(1)
    z_round(1, grad, 2)

    def blocks(ref, core):
        return jnp.concatenate(
            [ref[pl.ds(pl.multiple_of(h * 256 + core * 128, 128), 128), :] for h in range(2)], axis=0
        )

    def product(a, core, out):
        left = blocks(hid if a in (0, 2) else grad, core)

        tile = TILES[a]

        @pl.loop(0, COLS[a] // tile)
        def _(t):
            cols = pl.ds(pl.multiple_of(t * tile, 128), tile)
            if a == 0:
                out[:, cols] = dot(left, gathered[a][t])
            elif a == 2:
                out[:, cols] = dot(left, gathered[a][:, cols])
            else:
                out[:, cols] = dot_nt(left, gathered[a][cols, :])

    def mate_copy(a):
        return remote(lo[a], arrived[a], ms.at[a], mr.at[a], place.mate_at)

    def compute(a):
        product(a, 1 - place.c, lo[a])
        start(mate_copy(a))
        product(a, place.c, own[a])

    far_parts = (
        ((xs_f, xr_f, 0, 0, 768), (xs_q, xr_q, 1, 768, 384)),
        ((xs_o, xr_o, 2, 0, 384),),
        ((xs_u, xr_u, 3, 0, 1536),),
        ((xs_d, xr_d, 4, 0, 1536),),
    )

    def cross_copy(send, recv, k):
        return remote(send, recv, cs.at[k], cr.at[k], place.cross_at)

    there = pl.ds(pl.multiple_of((1 - place.h) * 128, 128), 128)
    here = pl.ds(pl.multiple_of(place.h * 128, 128), 128)

    def reduce_near(a):
        mate_copy(a).wait_recv()
        for send, recv, k, first, count in far_parts[a]:
            cols = pl.ds(first, count)
            send[...] = (own[a][there, cols] + arrived[a][there, cols]).astype(send.dtype)
            start(cross_copy(send, recv, k))
        final[a][...] = own[a][here, :] + arrived[a][here, :]

    def reduce_far(a):
        for send, recv, k, first, count in far_parts[a]:
            cross_copy(send, recv, k).wait_recv()
            final[a][:, first : first + count] += recv[...].astype(F32)

    z_done(0, hid)
    stage4(0)
    compute(0)
    z_round(1, grad, 3)
    stage2(2)
    stage1(3)
    reduce_near(0)
    hid_t[...] = hid[...].T
    z_done(1, grad)
    stage4(1)
    compute(1)
    reduce_near(1)
    stage3(2)

    mine = pl.ds(pl.multiple_of(place.o * 128, 128), 128)
    reduce_far(0)
    for j in range(3):
        cols = slice(j * 128, (j + 1) * 128)
        for part in range(2):
            at = slice(part * 384 + j * 128, part * 384 + (j + 1) * 128)
            hat, hat_inv = normalize(fq[:, at])
            hats[:, at] = hat
            invs[:, at] = jnp.broadcast_to(hat_inv, (128, 128))
            low = (hat * head_gain[part : part + 1, :]).astype(BF16)
            if part == 0:
                qlow[:, cols] = low
            else:
                kv[mine, cols] = low
    kv[mine, 384:768] = fq[:, 768:1152].astype(BF16)
    out_send(0, kv)
    stage2(3)
    reduce_far(1)
    alow[...] = fo[...].astype(BF16)
    out_relay(0, kv)
    stage4(2)
    compute(2)
    reduce_near(2)
    stage3(3)
    out_wait(0, kv)

    query_gain = jnp.zeros((1, 128), F32)
    for j in range(3):
        cols = slice(j * 128, (j + 1) * 128)
        vals = slice(384 + j * 128, 384 + (j + 1) * 128)
        query, incoming = qlow[:, cols], alow[:, cols]
        keys, values = kv[:, cols], kv[:, vals]
        scores = dot_nt(query, keys) * SCALE
        raised = jnp.exp(scores - jnp.max(scores, axis=-1, keepdims=True))
        weights = raised / jnp.sum(raised, axis=-1, keepdims=True)
        weights_low = weights.astype(BF16)
        att[mine, cols] = dot(weights_low, values).astype(BF16)
        slopes = dot_nt(incoming, values)
        centre = jnp.sum(weights * slopes, axis=-1, keepdims=True)
        score_grad = (weights * (slopes - centre)).astype(BF16)
        kvpart[:, cols] = dot_tn(score_grad, query) * SCALE
        kvpart[:, vals] = dot_tn(weights_low, incoming)
        query_grad = dot(score_grad, keys) * SCALE
        hat = hats[:, cols]
        query_gain = query_gain + jnp.sum(query_grad * hat, axis=0, keepdims=True)
        back = normalize_back(query_grad * head_gain[0:1, :], hat, invs[:, cols])
        qg[mine, cols] = back.astype(BF16)
    out_send(1, att)

    def kv_near(h):
        rows = pl.ds(pl.multiple_of(h * 256 + (1 - place.c) * 128, 128), 128)
        return remote(kvpart.at[rows], kvin.at[h], ks.at[h], kr.at[h], place.mate_at)

    kv_far = remote(kvs, kvr, ks.at[2], kr.at[2], place.cross_at)
    for h in range(2):
        start(kv_near(h))

    reduce_far(2)

    def before_tile(t):
        cols = pl.ds(pl.multiple_of(t * 512, 512), 512)
        before = fu[:, cols]
        return cols, before, 0.5 * (1.0 + lax.erf(before * ROOT_HALF))

    @pl.loop(0, 3)
    def _(t):
        cols, before, below = before_tile(t)
        act[mine, cols] = (before * below).astype(BF16)
        fu[:, cols] = below + before * jnp.exp(-0.5 * before * before) / ROOT_TWO_PI

    for h in range(2):
        kv_near(h).wait_recv()
    other = pl.ds(pl.multiple_of(place.cross * 128, 128), 128)
    kvs[...] = (kvpart[other, :] + kvin[1 - place.h]).astype(kvs.dtype)
    start(kv_far)
    out_send(2, act)
    stage4(3)
    compute(3)
    out_relay(1, att)
    reduce_near(3)
    kv_far.wait_recv()
    key_gain = jnp.zeros((1, 128), F32)
    for j in range(3):
        cols = slice(j * 128, (j + 1) * 128)
        keys = slice(384 + j * 128, 384 + (j + 1) * 128)
        vals = slice(768 + j * 128, 768 + (j + 1) * 128)
        key_grad = kvpart[mine, cols] + kvin[place.h, :, cols] + kvr[:, cols].astype(F32)
        hat = hats[:, keys]
        key_gain = key_gain + jnp.sum(key_grad * hat, axis=0, keepdims=True)
        back = normalize_back(key_grad * head_gain[1:2, :], hat, invs[:, keys])
        qg[mine, keys] = back.astype(BF16)
        value_grad = kvpart[mine, keys] + kvin[place.h, :, keys] + kvr[:, keys].astype(F32)
        qg[mine, vals] = value_grad.astype(BF16)
    out_send(4, qg)
    row = lax.broadcasted_iota(jnp.int32, (8, 128), 0)
    hz_out[...] = jnp.where(row == 0, query_gain, jnp.where(row == 1, key_gain, 0.0))
    fan_send("in", place.i, 8, hz_out, hz_in, vs.at[0], vr.at[0])

    def weight_product(a):
        tile = TILES[a]
        if a == 0:

            @pl.loop(0, 3)
            def _(t):
                pq[t] = dot(hid_t[...], qg[:, pl.ds(pl.multiple_of(t * tile, 128), tile)]).astype(BF16)
        elif a == 2:

            @pl.loop(0, 3)
            def _(t):
                cols = pl.ds(pl.multiple_of(t * tile, 128), tile)
                pu[:, cols] = dot(hid_t[...], bg[:, cols]).astype(BF16)
        else:
            left = att if a == 1 else act

            @pl.loop(0, COLS[a] // tile)
            def _(t):
                cols = pl.ds(pl.multiple_of(t * tile, 128), tile)
                partial[a][cols, :] = dot_tn(left[:, cols], grad[...]).astype(BF16)

    def back_place(a, k):
        rows, _ = SHARD[a]
        part = place.table[k][4]
        slot = (0, 1, 2, 3, 3, 4, 5, 6)[k]
        if part == "all":
            return returned[a].at[slot]
        if part == "low":
            return slots(a, returned[a].at[slot], pl.ds(0, SPLIT[a]))
        return slots(a, returned[a].at[slot], pl.ds(SPLIT[a], rows - SPLIT[a]))

    def back_copy(a, k):
        rows, _ = SHARD[a]
        _, target, _, slot, part = place.table[k]
        source = slots(a, partial[a], rows_of(slot, rows, SPLIT[a], part))
        return remote(source, back_place(a, k), ws.at[a, k], wr.at[a, k], {"dep": target})

    def b_send(a, *kinds):
        for k in kinds:
            start(back_copy(a, k))

    def b_add(a, *kinds):
        rows, _ = SHARD[a]
        for k in kinds:
            back_copy(a, k).wait_recv()
        _, _, slot, _, part = place.table[kinds[0]]
        at = slots(a, partial[a], rows_of(slot, rows, SPLIT[a], part))
        total = at[...].astype(F32)
        for k in kinds:
            total = total + back_place(a, k)[...].astype(F32)
        return at, total

    def b_merge(a, *kinds):
        at, total = b_add(a, *kinds)
        at[...] = total.astype(BF16)

    def back1(a):
        b_send(a, 7, 5, 6)

    def back2(a):
        b_merge(a, 7)
        b_send(a, 3, 4)
        b_merge(a, 5, 6)
        b_send(a, 2)

    def back3(a):
        b_merge(a, 3)
        b_send(a, 0)
        b_merge(a, 4)
        b_send(a, 1)

    def back4(a):
        _, total = b_add(a, 0, 1, 2)
        result[a][...] = total

    def to_in(which, send, recv, mine_ref, term):
        for b in range(2):
            rows = slice(b * 256, (b + 1) * 256)
            own0[:, :768] = term(rows)
            send[rows, :] = own0[:, :768].astype(BF16)

            @pl.when(place.i // 4 == b)
            def _():
                mine_ref[...] = own0[pl.ds(pl.multiple_of((place.i % 4) * 64, 64), 64), :768]

        zsum_send(which, send, recv)

    out_relay(2, act)
    out_wait(1, att)
    weight_product(1)
    back1(1)
    out_wait(2, act)
    weight_product(3)
    back1(3)
    out_relay(4, qg)
    reduce_far(3)

    @pl.loop(0, 3)
    def _(t):
        cols = pl.ds(pl.multiple_of(t * 512, 512), 512)
        bg[mine, cols] = (fd[:, cols] * fu[:, cols]).astype(BF16)

    out_send(3, bg)
    back2(1)
    to_in(2, zsend0, zin0, zown0, lambda r: dot(att[r, :], go[...]) + dot(act[r, :], gd[...]))
    out_wait(4, qg)
    weight_product(0)
    back1(0)
    back2(3)
    out_relay(3, bg)
    back3(1)
    out_wait(3, bg)
    weight_product(2)
    back1(2)
    back2(0)
    back3(3)

    def input_term(r):
        total = dot_nt(bg[r, :], gu[...])
        for part in range(3):
            total = total + dot_nt(qg[r, part * 384 : (part + 1) * 384], gq[part])
        return total

    to_in(3, zsend1, zin1, zown1, input_term)
    back2(2)
    back3(0)
    hd_out[...] = fan_total("in", place.i, 8, hz_out, hz_in, vs.at[0], vr.at[0])
    fan_send("dep", place.d, 8, hd_out, hd_in, vs.at[1], vr.at[1])
    lo_buf[...] = (tok[...].astype(F32) + zsum_total(2, zsend0, zin0, zown0)).astype(BF16)
    swap_start(2, lo_buf, lo_in, layer_out)

    input_grad = zsum_total(3, zsend1, zin1, zown1)
    scaled = input_grad * gain[...]
    first = jnp.sum(scaled, axis=1, keepdims=True)
    second = jnp.sum(scaled * normed[...], axis=1, keepdims=True)
    tot_out[...] = jnp.where(lane < 64, first, second)
    fan_send("out", place.o, 4, tot_out, tot_in, ss.at[1], sr.at[1])
    vz_out[...] = jnp.sum(input_grad * normed[...], axis=0, keepdims=True)
    fan_send("in", place.i, 8, vz_out, vz_in, vs.at[2], vr.at[2])
    back3(2)
    totals = fan_total("out", place.o, 4, tot_out, tot_in, ss.at[1], sr.at[1])
    centred = scaled - totals[:, :1] * (1.0 / 3072.0) - normed[...] * (totals[:, 64:65] * (1.0 / 3072.0))
    tg_buf[...] = (ups[...].astype(F32) + inverse[:, :1] * centred).astype(BF16)
    swap_start(3, tg_buf, tg_in, token_grad)
    vd_out[...] = fan_total("in", place.i, 8, vz_out, vz_in, vs.at[2], vr.at[2])
    fan_send("dep", place.d, 8, vd_out, vd_in, vs.at[3], vr.at[3])
    ho_out[...] = fan_total("dep", place.d, 8, hd_out, hd_in, vs.at[1], vr.at[1])
    fan_send("out", place.o, 4, ho_out, ho_in, ss.at[2], sr.at[2])
    back4(1)
    back4(3)
    back4(2)
    back4(0)
    head_grad[...] = fan_total("out", place.o, 4, ho_out, ho_in, ss.at[2], sr.at[2])[:2]
    swap_end(2, lo_buf, lo_in, layer_out)
    swap_end(3, tg_buf, tg_in, token_grad)
    gain_grad[...] = fan_total("dep", place.d, 8, vd_out, vd_in, vs.at[3], vr.at[3])
    for copy in pending:
        copy.wait_send()


def layer(tokens, gain, head_gain, upstream, wq, wo, wu, wd):
    shape = jax.ShapeDtypeStruct
    outs = [
        shape((64, 768), BF16), shape((64, 768), BF16), shape((1, 768), F32), shape((2, 128), F32),
        shape((3, 96, 384), F32), shape((48, 768), F32), shape((96, 1536), F32), shape((192, 768), F32),
    ]
    whole = pl.BlockSpec(memory_space=VMEM)
    far = [VMEM((128, 768), F32), VMEM((128, 384), BF16), VMEM((128, 384), BF16), VMEM((128, 1536), BF16), VMEM((128, 1536), BF16)]
    full = [VMEM((3, 768, 384), BF16), VMEM((384, 768), BF16), VMEM((768, 1536), BF16), VMEM((1536, 768), BF16)]
    scratch = full + [VMEM((512, 768), BF16), VMEM((512, 768), BF16), VMEM((64, 768), F32), VMEM((64, 128), F32)]
    scratch += [VMEM((128, n), F32) for n in COLS]
    scratch += [VMEM((64, 128), F32), VMEM((3, 64, 128), F32)]
    for _ in range(3):
        scratch += [VMEM((256, n), F32) for n in COLS]
    scratch += far + far
    scratch += [VMEM((512, n), BF16) for n in (768, 384, 1536, 1536, 1152)]
    scratch += [VMEM((128, 384), BF16), VMEM((128, 384), BF16), VMEM((128, 768), F32), VMEM((128, 768), F32)]
    scratch += [VMEM((512, 768), F32), VMEM((2, 128, 768), F32), VMEM((128, 768), BF16), VMEM((128, 768), BF16)]
    scratch += [VMEM((64, 768), BF16)] * 2 + [VMEM((768, 512), BF16)] + [VMEM((64, 768), BF16)] * 4
    scratch += full + [VMEM((7, 3, 96, 384), BF16)] + [VMEM((7, rows, cols), BF16) for rows, cols in SHARD[1:]]
    scratch += [VMEM((512, 768), BF16)] * 2 + [VMEM((7, 64, 768), BF16)] * 2 + [VMEM((64, 768), F32)] * 2
    scratch += [VMEM((64, 128), F32), VMEM((3, 64, 128), F32)]
    scratch += [VMEM((1, 768), F32), VMEM((7, 1, 768), F32)] * 2
    scratch += [VMEM((8, 128), F32), VMEM((7, 8, 128), F32)] * 2
    scratch += [VMEM((8, 128), F32), VMEM((3, 8, 128), F32)]
    dma = pltpu.SemaphoreType.DMA
    scratch += [dma((4, 8)), dma((4, 8)), dma((4,)), dma((4, 8)), dma((4, 8)), dma((3, 3)), dma((3, 3))]
    scratch += [dma((4,)), dma((4,)), dma((5,)), dma((5,)), dma((5, 3)), dma((5, 3)), dma((3,)), dma((3,))]
    scratch += [dma((4, 8)), dma((4, 8)), dma((4, 7)), dma((4, 7)), dma((4,)), dma((4,))]
    return pl.pallas_call(
        layer_kernel,
        out_shape=outs,
        in_specs=[whole] * 4 + [pl.BlockSpec(memory_space=pl.ANY)] * 4,
        out_specs=[whole] * len(outs),
        scratch_shapes=scratch,
        compiler_params=pltpu.CompilerParams(collective_id=1, has_side_effects=True, vmem_limit_bytes=62 * 2**20),
        cost_estimate=pl.CostEstimate(flops=11 * 10**9, bytes_accessed=10**7, transcendentals=10**6),
    )(tokens, gain, head_gain, upstream, wq, wo, wu, wd)


def body(tokens, norm_gain, qkv_weight, head_gain, out_weight, up_weight, down_weight, upstream):
    layer_out, token_grad, gain_grad, head_grad, dq, do, du, dd = layer(
        tokens[0], norm_gain[None], head_gain, upstream[0],
        jnp.transpose(qkv_weight, (1, 0, 2)), out_weight, up_weight, down_weight,
    )
    return (
        layer_out[None], token_grad[None], gain_grad[0], head_grad,
        jnp.transpose(dq, (1, 0, 2)), do, du, dd,
    )


def solution(mesh):
    placed = (
        P("dep", "in", "out"),
        P("out"),
        P(("out", "dep"), None, "in"),
        P(),
        P(("in", "dep"), "out"),
        P(("out", "dep"), "in"),
        P(("in", "dep"), "out"),
        P("dep", "in", "out"),
    )
    return jax.shard_map(
        body,
        mesh=mesh,
        in_specs=placed,
        out_specs=(
            P("dep", "in", "out"),
            P("dep", "in", "out"),
            P("out"),
            P(),
            P(("out", "dep"), None, "in"),
            P(("in", "dep"), "out"),
            P(("out", "dep"), "in"),
            P(("in", "dep"), "out"),
        ),
        check_vma=False,
    )
```

```python
import math

import jax
import jax.numpy as jnp
from jax import lax
from jax.experimental import pallas as pl
from jax.experimental.pallas import tpu as pltpu
from jax.sharding import PartitionSpec as P

MESH = pl.DeviceIdType.MESH
EPSILON = 1e-06
ROOT_HALF = 1.0 / math.sqrt(2.0)
ROOT_TWO_PI = math.sqrt(2.0 * math.pi)
SCALE = 128.0 ** (-0.5)
F32 = jnp.float32
BF16 = jnp.bfloat16
VMEM = pltpu.VMEM

TILES = (384, 384, 512, 512)
COLS = (1152, 384, 1536, 1536)
SHARD = ((96, 1152), (48, 768), (96, 1536), (192, 768))
SPLIT = (48, 32, 48, 96)
RING = (1, 7, 2, 6, 3, 5, 4)


def remote(src, dst, send, recv, device):
    return pltpu.make_async_remote_copy(
        src_ref=src, dst_ref=dst, send_sem=send, recv_sem=recv, device_id=device, device_id_type=MESH
    )


class Place:
    def __init__(self):
        self.i = lax.axis_index("in")
        self.o = lax.axis_index("out")
        self.d = lax.axis_index("dep")
        d = self.d
        x, y = d // 2, d % 2
        right, left, far = (x + 1) % 4, (x + 3) % 4, (x + 2) % 4
        self.me = d
        self.r, self.l, self.f = right * 2 + y, left * 2 + y, far * 2 + y
        self.p = x * 2 + 1 - y
        self.rp, self.lp, self.fp = right * 2 + 1 - y, left * 2 + 1 - y, far * 2 + 1 - y
        self.h, self.c = self.o // 2, self.o % 2
        self.mate = self.h * 2 + 1 - self.c
        self.cross = (1 - self.h) * 2 + self.c
        self.mate_at = {"out": self.mate}
        self.cross_at = {"out": self.cross, "dep": self.p}
        self.diag_at = {"out": (1 - self.h) * 2 + 1 - self.c, "dep": self.p}
        self.diag = (1 - self.h) * 2 + 1 - self.c
        self.table = (
            (self.r, self.l, self.me, self.l, "all"),
            (self.l, self.r, self.me, self.r, "all"),
            (self.p, self.p, self.me, self.p, "all"),
            (self.r, self.l, self.l, self.f, "low"),
            (self.l, self.r, self.r, self.f, "high"),
            (self.r, self.l, self.p, self.lp, "all"),
            (self.l, self.r, self.p, self.rp, "all"),
            (self.p, self.p, self.f, self.fp, "all"),
        )


def rows_of(slot, rows, split, part):
    start = slot * rows
    if part == "all":
        return pl.ds(pl.multiple_of(start, 16), rows)
    if part == "low":
        return pl.ds(pl.multiple_of(start, 16), split)
    return pl.ds(pl.multiple_of(start + split, 16), rows - split)


def greet(place):
    barrier = pltpu.get_barrier_semaphore()
    for k in range(1, 8):
        pl.semaphore_signal(barrier, inc=1, device_id={"in": (place.i + k) % 8}, device_id_type=MESH)
        pl.semaphore_signal(barrier, inc=1, device_id={"dep": (place.d + k) % 8}, device_id_type=MESH)
    for peer in (place.mate_at, place.cross_at, place.diag_at):
        pl.semaphore_signal(barrier, inc=1, device_id=peer, device_id_type=MESH)
    pl.semaphore_wait(barrier, 17)


def dot(a, b):
    return lax.dot_general(a, b, (((1,), (0,)), ((), ())), preferred_element_type=F32)


def dot_nt(a, b):
    return lax.dot_general(a, b, (((1,), (1,)), ((), ())), preferred_element_type=F32)


def dot_tn(a, b):
    return lax.dot_general(a, b, (((0,), (0,)), ((), ())), preferred_element_type=F32)


def normalize(values):
    average = jnp.mean(values, axis=-1, keepdims=True)
    spread = jnp.mean(values * values, axis=-1, keepdims=True) - average * average
    inverse = lax.rsqrt(spread + EPSILON)
    return ((values - average) * inverse, inverse)


def normalize_back(incoming, normed, inverse):
    first = jnp.mean(incoming, axis=-1, keepdims=True)
    second = jnp.mean(incoming * normed, axis=-1, keepdims=True)
    return inverse * (incoming - first - normed * second)


def layer_kernel(
    tokens, gain, head_gain, upstream, wq, wo, wu, wd,
    layer_out, token_grad, gain_grad, head_grad, dq, do, du, dd,
    gq, go, gu, gd, hid, grad, normed, inverse, fq, fo, fu, fd,
    stat_out, stat_in, away0, away1, away2, away3, home0, home1, home2, home3, in0, in1, in2, in3,
    xs_f, xs_q, xs_o, xs_u, xs_d, xr_f, xr_q, xr_o, xr_u, xr_d,
    kv, att, act, bg, qg, qlow, alow, hats, invs, kvpart, kvin, kvs, kvr,
    tok, ups, hid_t, lo_buf, lo_in, tg_buf, tg_in,
    pq, po, pu, pd, rq, ro, ru, rd, zsend0, zin0, zown0, ring_out, ring_in,
    tot_out, tot_in, vz_out, vz_in, vd_out, vd_in, hz_out, hz_in, hd_out, hd_in, ho_out, ho_in,
    gs, gr, gl, zs, zr, ss, sr, ms, mr, cs, cr, bs, br, ks, kr, ws, wr, vs, vr, es, er,
):
    place = Place()
    shards = (wq, wo, wu, wd)
    gathered = (gq, go, gu, gd)
    away, home, arrived, final = (away0, away1, away2, away3), (home0, home1, home2, home3), (in0, in1, in2, in3), (fq, fo, fu, fd)
    partial, returned, result = (pq, po, pu, pd), (rq, ro, ru, rd), (dq, do, du, dd)
    greet(place)
    pending = []

    def start(copy):
        copy.start()
        pending.append(copy)

    def local(src, dst, sem):
        copy = pltpu.make_async_copy(src, dst, sem)
        copy.start()
        return copy

    def slots(a, ref, rows):
        return ref.at[:, rows] if a == 0 else ref.at[rows]

    def gather_copy(a, k, receive=False):
        rows, _ = SHARD[a]
        target, _, mine, theirs, part = place.table[k]
        ref = slots(a, gathered[a], rows_of(theirs if receive else mine, rows, SPLIT[a], part))
        source = ref if receive or k > 2 else shards[a]
        return remote(source, ref, gs.at[a, k], gr.at[a, k], {"dep": target})

    def g_send(a, *kinds):
        for k in kinds:
            start(gather_copy(a, k))

    def g_wait(a, *kinds):
        for k in kinds:
            gather_copy(a, k, True).wait_recv()

    own_copies = [None] * 4

    def stage1(a):
        g_send(a, 0, 1, 2)
        rows, _ = SHARD[a]
        own_copies[a] = local(shards[a], slots(a, gathered[a], rows_of(place.me, rows, 0, "all")), gl.at[a])

    def stage2(a):
        g_wait(a, 0)
        g_send(a, 3)
        g_wait(a, 1)
        g_send(a, 4)
        g_wait(a, 2)
        g_send(a, 5, 6)

    def stage3(a):
        g_wait(a, 3, 4)
        g_send(a, 7)

    def stage4(a):
        g_wait(a, 5, 6, 7)
        own_copies[a].wait()

    def z_slot(ref, index):
        return ref.at[pl.ds(pl.multiple_of(index * 64, 64), 64)]

    def z_ring_copy(which, kind, ref, receive=False):
        turn = kind % 4
        if kind < 4:
            target, slot = (place.i + 1) % 8, (place.i + (7 if receive else 8) - turn) % 8
        else:
            target, slot = (place.i + 7) % 8, (place.i + (1 if receive else 0) + turn) % 8
        first = 32 if kind == 7 else 0
        at = ref.at[pl.ds(pl.multiple_of(slot * 64 + first, 32), 32 if turn == 3 else 64)]
        return remote(at, at, zs.at[which, kind], zr.at[which, kind], {"in": target})

    def z_round(which, ref, turn):
        for way in (0, 4):
            if turn > 0:
                z_ring_copy(which, way + turn - 1, ref, True).wait_recv()
            start(z_ring_copy(which, way + turn, ref))

    def z_done(which, ref):
        for way in (0, 4):
            z_ring_copy(which, way + 3, ref, True).wait_recv()

    def zsum_copy(which, k, send, recv):
        to = (place.i + k) % 8
        return remote(z_slot(send, to), recv.at[k - 1], zs.at[which, k - 1], zr.at[which, k - 1], {"in": to})

    def zsum_send(which, send, recv):
        for k in RING:
            start(zsum_copy(which, k, send, recv))

    def zsum_total(which, send, recv, mine):
        total = mine[...]
        for k in RING:
            zsum_copy(which, k, send, recv).wait_recv()
            total = total + recv[k - 1].astype(F32)
        return total

    def fan_copy(axis, index, size, k, send, recv, sem_s, sem_r):
        if axis == "out":
            peer = (place.mate_at, place.cross_at, place.diag_at)[k - 1]
        else:
            peer = {axis: (index + k) % size}
        return remote(send, recv.at[k - 1], sem_s.at[k - 1], sem_r.at[k - 1], peer)

    def fan_send(axis, index, size, send, recv, sem_s, sem_r):
        for k in range(1, size):
            start(fan_copy(axis, index, size, k, send, recv, sem_s, sem_r))

    def fan_total(axis, index, size, send, recv, sem_s, sem_r):
        total = send[...]
        for k in range(1, size):
            fan_copy(axis, index, size, k, send, recv, sem_s, sem_r).wait_recv()
            total = total + recv[k - 1]
        return total

    def out_rows(ref, index):
        return ref.at[pl.ds(pl.multiple_of(index * 128, 128), 128)]

    def out_copy(which, k, ref, receive=False):
        sent = (place.o, place.o, place.cross)[k]
        got = (place.mate, place.cross, place.diag)[k]
        target = (place.mate_at, place.cross_at, place.mate_at)[k]
        rows = out_rows(ref, got if receive else sent)
        return remote(rows, rows, bs.at[which, k], br.at[which, k], target)

    def out_send(which, ref):
        start(out_copy(which, 1, ref))
        start(out_copy(which, 0, ref))

    def out_relay(which, ref):
        out_copy(which, 1, ref, True).wait_recv()
        start(out_copy(which, 2, ref))

    def out_wait(which, ref):
        out_copy(which, 0, ref, True).wait_recv()
        out_copy(which, 2, ref, True).wait_recv()

    def swap_copy(k, source, landing):
        return remote(source, landing, es.at[k], er.at[k], {"dep": place.p})

    def swap_start(k, source, landing, result):
        @pl.when(place.h == 1)
        def _():
            swap_copy(k, source, landing).start()

        @pl.when(place.h == 0)
        def _():
            result[...] = source[...]

    def swap_end(k, source, landing, result):
        @pl.when(place.h == 1)
        def _():
            swap_copy(k, source, landing).wait()
            if result is not landing:
                result[...] = landing[...]

    swap_start(0, tokens, tok, tok)
    swap_start(1, upstream, ups, ups)
    stage1(0)
    stage1(1)
    swap_end(0, tokens, tok, tok)

    wide = tok[...].astype(F32)
    lane = lax.broadcasted_iota(jnp.int32, (64, 128), 1)
    total = jnp.sum(wide, axis=1, keepdims=True)
    square = jnp.sum(wide * wide, axis=1, keepdims=True)
    stat_out[...] = jnp.where(lane < 64, total, square)
    fan_send("out", place.o, 4, stat_out, stat_in, ss.at[0], sr.at[0])
    swap_end(1, upstream, ups, ups)
    z_slot(grad, place.i)[...] = ups[...]
    stats = fan_total("out", place.o, 4, stat_out, stat_in, ss.at[0], sr.at[0])
    average = stats[:, :1] * (1.0 / 3072.0)
    spread = stats[:, 64:65] * (1.0 / 3072.0) - average * average
    inv = lax.rsqrt(spread + EPSILON)
    norm = (wide - average) * inv
    normed[...] = norm
    inverse[...] = jnp.broadcast_to(inv, (64, 128))
    z_slot(hid, place.i)[...] = (norm * gain[...]).astype(BF16)
    z_round(0, hid, 0)
    z_round(1, grad, 0)
    stage2(0)
    z_round(0, hid, 1)
    stage2(1)
    stage1(2)
    z_round(0, hid, 2)
    stage3(0)
    z_round(0, hid, 3)
    z_round(1, grad, 1)
    stage3(1)

    def product(a, half, out):
        left = (hid if a in (0, 2) else grad)[pl.ds(pl.multiple_of(half * 256, 256), 256), :]
        tile = TILES[a]

        @pl.loop(0, COLS[a] // tile)
        def _(t):
            cols = pl.ds(pl.multiple_of(t * tile, 128), tile)
            if a == 0:
                out[:, cols] = dot(left, gathered[a][t])
            elif a == 2:
                out[:, cols] = dot(left, gathered[a][:, cols])
            else:
                out[:, cols] = dot_nt(left, gathered[a][cols, :])

    theirs = pl.ds(pl.multiple_of((1 - place.c) * 128, 128), 128)
    ours = pl.ds(pl.multiple_of(place.c * 128, 128), 128)

    def mate_copy(a, k):
        return remote(
            (away, home)[k][a].at[theirs], arrived[a].at[pl.ds(k * 128, 128)], ms.at[a, k], mr.at[a, k], place.mate_at
        )

    far_parts = (
        ((xs_f, xr_f, 0, 0, 768), (xs_q, xr_q, 1, 768, 384)),
        ((xs_o, xr_o, 2, 0, 384),),
        ((xs_u, xr_u, 3, 0, 1536),),
        ((xs_d, xr_d, 4, 0, 1536),),
    )

    def cross_copy(send, recv, k):
        return remote(send, recv, cs.at[k], cr.at[k], place.cross_at)

    def compute(a):
        product(a, 1 - place.h, away[a])
        mate_copy(a, 0).start()
        product(a, place.h, home[a])
        mate_copy(a, 1).start()
        mate_copy(a, 0).wait_recv()
        for send, recv, k, first, count in far_parts[a]:
            cols = slice(first, first + count)
            send[...] = (away[a][ours, cols] + arrived[a][:128, cols]).astype(send.dtype)
            start(cross_copy(send, recv, k))

    def reduce_far(a):
        mate_copy(a, 1).wait_recv()
        for send, recv, k, first, count in far_parts[a]:
            cols = slice(first, first + count)
            cross_copy(send, recv, k).wait_recv()
            final[a][:, cols] = home[a][ours, cols] + arrived[a][128:, cols] + recv[...].astype(F32)
        for k in range(2):
            mate_copy(a, k).wait_send()

    z_done(0, hid)
    stage4(0)
    compute(0)
    z_round(1, grad, 2)
    stage2(2)
    stage1(3)
    z_round(1, grad, 3)
    stage3(2)
    z_done(1, grad)
    stage4(1)
    compute(1)
    hid_t[...] = hid[...].T

    mine = pl.ds(pl.multiple_of(place.o * 128, 128), 128)
    reduce_far(0)
    for j in range(3):
        cols = slice(j * 128, (j + 1) * 128)
        for part in range(2):
            at = slice(part * 384 + j * 128, part * 384 + (j + 1) * 128)
            hat, hat_inv = normalize(fq[:, at])
            hats[:, at] = hat
            invs[:, at] = jnp.broadcast_to(hat_inv, (128, 128))
            low = (hat * head_gain[part : part + 1, :]).astype(BF16)
            if part == 0:
                qlow[:, cols] = low
            else:
                kv[mine, cols] = low
    kv[mine, 384:768] = fq[:, 768:1152].astype(BF16)
    out_send(0, kv)
    stage4(2)
    compute(2)
    out_relay(0, kv)
    reduce_far(1)
    alow[...] = fo[...].astype(BF16)
    stage2(3)
    out_wait(0, kv)

    def attend(j):
        cols = slice(j * 128, (j + 1) * 128)
        vals = slice(384 + j * 128, 384 + (j + 1) * 128)
        query, incoming = qlow[:, cols], alow[:, cols]
        keys, values = kv[:, cols], kv[:, vals]
        scores = dot_nt(query, keys) * SCALE
        raised = jnp.exp(scores - jnp.max(scores, axis=-1, keepdims=True))
        weights = raised / jnp.sum(raised, axis=-1, keepdims=True)
        weights_low = weights.astype(BF16)
        att[mine, cols] = dot(weights_low, values).astype(BF16)
        slopes = dot_nt(incoming, values)
        centre = jnp.sum(weights * slopes, axis=-1, keepdims=True)
        score_grad = (weights * (slopes - centre)).astype(BF16)
        kvpart[:, cols] = dot_tn(score_grad, query) * SCALE
        kvpart[:, vals] = dot_tn(weights_low, incoming)
        query_grad = dot(score_grad, keys) * SCALE
        hat = hats[:, cols]
        gain_part = jnp.sum(query_grad * hat, axis=0, keepdims=True)
        back = normalize_back(query_grad * head_gain[0:1, :], hat, invs[:, cols])
        qg[mine, cols] = back.astype(BF16)
        return gain_part

    def kv_near(h):
        rows = pl.ds(pl.multiple_of(h * 256 + (1 - place.c) * 128, 128), 128)
        return remote(kvpart.at[rows], kvin.at[h], ks.at[h], kr.at[h], place.mate_at)

    kv_far = remote(kvs, kvr, ks.at[2], kr.at[2], place.cross_at)
    def before_tile(t):
        cols = pl.ds(pl.multiple_of(t * 512, 512), 512)
        before = fu[:, cols]
        return cols, before, 0.5 * (1.0 + lax.erf(before * ROOT_HALF))

    query_gain = attend(0)
    stage3(3)
    query_gain = query_gain + attend(1)

    reduce_far(2)

    @pl.loop(0, 3)
    def _(t):
        cols, before, below = before_tile(t)
        act[mine, cols] = (before * below).astype(BF16)
        fu[:, cols] = below + before * jnp.exp(-0.5 * before * before) / ROOT_TWO_PI

    out_send(2, act)
    query_gain = query_gain + attend(2)
    for h in range(2):
        start(kv_near(h))
    out_send(1, att)
    for h in range(2):
        kv_near(h).wait_recv()
    other = pl.ds(pl.multiple_of(place.cross * 128, 128), 128)
    kvs[...] = (kvpart[other, :] + kvin[1 - place.h]).astype(kvs.dtype)
    start(kv_far)
    stage4(3)
    compute(3)
    def weight_product(a):
        tile = TILES[a]
        if a == 0:

            @pl.loop(0, 3)
            def _(t):
                pq[t] = dot(hid_t[...], qg[:, pl.ds(pl.multiple_of(t * tile, 128), tile)]).astype(BF16)
        elif a == 2:

            @pl.loop(0, 3)
            def _(t):
                cols = pl.ds(pl.multiple_of(t * tile, 128), tile)
                pu[:, cols] = dot(hid_t[...], bg[:, cols]).astype(BF16)
        else:
            left = att if a == 1 else act

            @pl.loop(0, COLS[a] // tile)
            def _(t):
                cols = pl.ds(pl.multiple_of(t * tile, 128), tile)
                partial[a][cols, :] = dot_tn(left[:, cols], grad[...]).astype(BF16)

    def back_place(a, k):
        rows, _ = SHARD[a]
        part = place.table[k][4]
        slot = (0, 1, 2, 3, 3, 4, 5, 6)[k]
        if part == "all":
            return returned[a].at[slot]
        if part == "low":
            return slots(a, returned[a].at[slot], pl.ds(0, SPLIT[a]))
        return slots(a, returned[a].at[slot], pl.ds(SPLIT[a], rows - SPLIT[a]))

    def back_copy(a, k):
        rows, _ = SHARD[a]
        _, target, _, slot, part = place.table[k]
        source = slots(a, partial[a], rows_of(slot, rows, SPLIT[a], part))
        return remote(source, back_place(a, k), ws.at[a, k], wr.at[a, k], {"dep": target})

    def b_send(a, *kinds):
        for k in kinds:
            start(back_copy(a, k))

    def b_add(a, *kinds):
        rows, _ = SHARD[a]
        for k in kinds:
            back_copy(a, k).wait_recv()
        _, _, slot, _, part = place.table[kinds[0]]
        at = slots(a, partial[a], rows_of(slot, rows, SPLIT[a], part))
        total = at[...].astype(F32)
        for k in kinds:
            total = total + back_place(a, k)[...].astype(F32)
        return at, total

    def b_merge(a, *kinds):
        at, total = b_add(a, *kinds)
        at[...] = total.astype(BF16)

    def back1(a):
        b_send(a, 7, 5, 6)

    def back2(a):
        b_merge(a, 7)
        b_send(a, 3, 4)
        b_merge(a, 5, 6)
        b_send(a, 2)

    def back3(a):
        b_merge(a, 3)
        b_send(a, 0)
        b_merge(a, 4)
        b_send(a, 1)

    def back4(a):
        _, total = b_add(a, 0, 1, 2)
        result[a][...] = total

    def to_in(which, send, recv, mine_ref, term):
        for b in range(2):
            rows = slice(b * 256, (b + 1) * 256)
            home0[:, :768] = term(rows)
            send[rows, :] = home0[:, :768].astype(BF16)

            @pl.when(place.i // 4 == b)
            def _():
                mine_ref[...] = home0[pl.ds(pl.multiple_of((place.i % 4) * 64, 64), 64), :768]

        zsum_send(which, send, recv)

    def block_of(index):
        index = index % 8
        rows = pl.ds(pl.multiple_of((index % 4) * 64, 64), 64)
        return away2.at[rows, pl.ds(pl.multiple_of((index // 4) * 768, 128), 768)]

    def ring_copy(way, step):
        target = (place.i + (1, 7)[way]) % 8
        rows = (pl.ds(0, 32), pl.ds(32, 32))[way] if step == 0 else pl.ds(0, 64)
        at = (way, step, rows)
        return remote(ring_out.at[at], ring_in.at[at], zs.at[3, way * 4 + step], zr.at[3, way * 4 + step], {"in": target})

    def ring_step(step):
        for way in range(2):
            block = block_of(place.i + (4 - step, 4 + step)[way])
            if step == 0:
                ring_out[way, 0] = block[...].astype(BF16)
            else:
                ring_copy(way, step - 1).wait_recv()
                if step == 1:
                    half = (slice(0, 32), slice(32, 64))[way]
                    block[half, :] += ring_in[way, 0, half, :].astype(F32)
                    ring_out[way, 1] = block[...].astype(BF16)
                else:
                    ring_out[way, step] = (block[...] + ring_in[way, step - 1].astype(F32)).astype(BF16)
            start(ring_copy(way, step))

    def ring_total():
        total = block_of(place.i)[...]
        for way in range(2):
            ring_copy(way, 3).wait_recv()
            total = total + ring_in[way, 3].astype(F32)
        return total

    out_relay(2, act)
    out_wait(2, act)
    weight_product(3)
    back1(3)
    out_relay(1, att)
    kv_far.wait_recv()
    key_gain = jnp.zeros((1, 128), F32)
    for j in range(3):
        cols = slice(j * 128, (j + 1) * 128)
        keys = slice(384 + j * 128, 384 + (j + 1) * 128)
        vals = slice(768 + j * 128, 768 + (j + 1) * 128)
        key_grad = kvpart[mine, cols] + kvin[place.h, :, cols] + kvr[:, cols].astype(F32)
        hat = hats[:, keys]
        key_gain = key_gain + jnp.sum(key_grad * hat, axis=0, keepdims=True)
        back = normalize_back(key_grad * head_gain[1:2, :], hat, invs[:, keys])
        qg[mine, keys] = back.astype(BF16)
        value_grad = kvpart[mine, keys] + kvin[place.h, :, keys] + kvr[:, keys].astype(F32)
        qg[mine, vals] = value_grad.astype(BF16)
    out_send(4, qg)
    row = lax.broadcasted_iota(jnp.int32, (8, 128), 0)
    hz_out[...] = jnp.where(row == 0, query_gain, jnp.where(row == 1, key_gain, 0.0))
    fan_send("in", place.i, 8, hz_out, hz_in, vs.at[0], vr.at[0])

    out_wait(1, att)
    weight_product(1)
    back1(1)
    back2(3)
    to_in(2, zsend0, zin0, zown0, lambda r: dot(att[r, :], go[...]) + dot(act[r, :], gd[...]))
    reduce_far(3)

    @pl.loop(0, 3)
    def _(t):
        cols = pl.ds(pl.multiple_of(t * 512, 512), 512)
        bg[mine, cols] = (fd[:, cols] * fu[:, cols]).astype(BF16)

    out_send(3, bg)
    back2(1)
    out_relay(4, qg)
    out_wait(4, qg)
    weight_product(0)
    back1(0)
    back3(3)
    for b in range(2):
        rows = slice(b * 256, (b + 1) * 256)
        away2[:, b * 768 : (b + 1) * 768] = sum(
            dot_nt(qg[rows, part * 384 : (part + 1) * 384], gq[part]) for part in range(3)
        )
    back2(0)
    out_relay(3, bg)
    out_wait(3, bg)
    weight_product(2)
    back1(2)
    for b in range(2):
        rows = slice(b * 256, (b + 1) * 256)
        away2[:, b * 768 : (b + 1) * 768] += dot_nt(bg[rows, :], gu[...])
    ring_step(0)
    back3(1)
    back3(0)
    ring_step(1)
    back2(2)
    ring_step(2)
    hd_out[...] = fan_total("in", place.i, 8, hz_out, hz_in, vs.at[0], vr.at[0])
    fan_send("dep", place.d, 8, hd_out, hd_in, vs.at[1], vr.at[1])
    lo_buf[...] = (tok[...].astype(F32) + zsum_total(2, zsend0, zin0, zown0)).astype(BF16)
    swap_start(2, lo_buf, lo_in, layer_out)
    ring_step(3)
    back3(2)

    input_grad = ring_total()
    scaled = input_grad * gain[...]
    first = jnp.sum(scaled, axis=1, keepdims=True)
    second = jnp.sum(scaled * normed[...], axis=1, keepdims=True)
    tot_out[...] = jnp.where(lane < 64, first, second)
    fan_send("out", place.o, 4, tot_out, tot_in, ss.at[1], sr.at[1])
    vz_out[...] = jnp.sum(input_grad * normed[...], axis=0, keepdims=True)
    fan_send("in", place.i, 8, vz_out, vz_in, vs.at[2], vr.at[2])
    back4(1)
    back4(3)
    totals = fan_total("out", place.o, 4, tot_out, tot_in, ss.at[1], sr.at[1])
    centred = scaled - totals[:, :1] * (1.0 / 3072.0) - normed[...] * (totals[:, 64:65] * (1.0 / 3072.0))
    tg_buf[...] = (ups[...].astype(F32) + inverse[:, :1] * centred).astype(BF16)
    swap_start(3, tg_buf, tg_in, token_grad)
    vd_out[...] = fan_total("in", place.i, 8, vz_out, vz_in, vs.at[2], vr.at[2])
    fan_send("dep", place.d, 8, vd_out, vd_in, vs.at[3], vr.at[3])
    ho_out[...] = fan_total("dep", place.d, 8, hd_out, hd_in, vs.at[1], vr.at[1])
    fan_send("out", place.o, 4, ho_out, ho_in, ss.at[2], sr.at[2])
    back4(0)
    back4(2)
    head_grad[...] = fan_total("out", place.o, 4, ho_out, ho_in, ss.at[2], sr.at[2])[:2]
    swap_end(2, lo_buf, lo_in, layer_out)
    swap_end(3, tg_buf, tg_in, token_grad)
    gain_grad[...] = fan_total("dep", place.d, 8, vd_out, vd_in, vs.at[3], vr.at[3])
    for copy in pending:
        copy.wait_send()


def layer(tokens, gain, head_gain, upstream, wq, wo, wu, wd):
    shape = jax.ShapeDtypeStruct
    outs = [
        shape((64, 768), BF16), shape((64, 768), BF16), shape((1, 768), F32), shape((2, 128), F32),
        shape((3, 96, 384), F32), shape((48, 768), F32), shape((96, 1536), F32), shape((192, 768), F32),
    ]
    whole = pl.BlockSpec(memory_space=VMEM)
    far = [VMEM((128, 768), F32), VMEM((128, 384), BF16), VMEM((128, 384), BF16), VMEM((128, 1536), BF16), VMEM((128, 1536), BF16)]
    full = [VMEM((3, 768, 384), BF16), VMEM((384, 768), BF16), VMEM((768, 1536), BF16), VMEM((1536, 768), BF16)]
    scratch = full + [VMEM((512, 768), BF16), VMEM((512, 768), BF16), VMEM((64, 768), F32), VMEM((64, 128), F32)]
    scratch += [VMEM((128, n), F32) for n in COLS]
    scratch += [VMEM((64, 128), F32), VMEM((3, 64, 128), F32)]
    for _ in range(3):
        scratch += [VMEM((256, n), F32) for n in COLS]
    scratch += far + far
    scratch += [VMEM((512, n), BF16) for n in (768, 384, 1536, 1536, 1152)]
    scratch += [VMEM((128, 384), BF16), VMEM((128, 384), BF16), VMEM((128, 768), F32), VMEM((128, 768), F32)]
    scratch += [VMEM((512, 768), F32), VMEM((2, 128, 768), F32), VMEM((128, 768), BF16), VMEM((128, 768), BF16)]
    scratch += [VMEM((64, 768), BF16)] * 2 + [VMEM((768, 512), BF16)] + [VMEM((64, 768), BF16)] * 4
    scratch += full + [VMEM((7, 3, 96, 384), BF16)] + [VMEM((7, rows, cols), BF16) for rows, cols in SHARD[1:]]
    scratch += [VMEM((512, 768), BF16), VMEM((7, 64, 768), BF16), VMEM((64, 768), F32)] + [VMEM((2, 4, 64, 768), BF16)] * 2
    scratch += [VMEM((64, 128), F32), VMEM((3, 64, 128), F32)]
    scratch += [VMEM((1, 768), F32), VMEM((7, 1, 768), F32)] * 2
    scratch += [VMEM((8, 128), F32), VMEM((7, 8, 128), F32)] * 2
    scratch += [VMEM((8, 128), F32), VMEM((3, 8, 128), F32)]
    dma = pltpu.SemaphoreType.DMA
    scratch += [dma((4, 8)), dma((4, 8)), dma((4,)), dma((4, 8)), dma((4, 8)), dma((3, 3)), dma((3, 3))]
    scratch += [dma((4, 2)), dma((4, 2)), dma((5,)), dma((5,)), dma((5, 3)), dma((5, 3)), dma((3,)), dma((3,))]
    scratch += [dma((4, 8)), dma((4, 8)), dma((4, 7)), dma((4, 7)), dma((4,)), dma((4,))]
    return pl.pallas_call(
        layer_kernel,
        out_shape=outs,
        in_specs=[whole] * 4 + [pl.BlockSpec(memory_space=pl.ANY)] * 4,
        out_specs=[whole] * len(outs),
        scratch_shapes=scratch,
        compiler_params=pltpu.CompilerParams(collective_id=1, has_side_effects=True, vmem_limit_bytes=62 * 2**20),
        cost_estimate=pl.CostEstimate(flops=11 * 10**9, bytes_accessed=10**7, transcendentals=10**6),
    )(tokens, gain, head_gain, upstream, wq, wo, wu, wd)


def settle_kernel(*refs):
    sources, targets, sems = refs[:8], refs[8:16], refs[16]
    copies = [pltpu.make_async_copy(a, b, sems.at[k]) for k, (a, b) in enumerate(zip(sources, targets))]
    for copy in copies:
        copy.start()
    for copy in copies:
        copy.wait()


def settle(*arrays):
    anywhere = pl.BlockSpec(memory_space=pl.ANY)
    return pl.pallas_call(
        settle_kernel,
        out_shape=[jax.ShapeDtypeStruct(a.shape, a.dtype) for a in arrays],
        in_specs=[anywhere] * 8,
        out_specs=[anywhere] * 8,
        scratch_shapes=[pltpu.SemaphoreType.DMA((8,))],
        cost_estimate=pl.CostEstimate(flops=0, bytes_accessed=8 * 10**6, transcendentals=0),
    )(*arrays)


def body(tokens, norm_gain, qkv_weight, head_gain, out_weight, up_weight, down_weight, upstream):
    layer_out, token_grad, gain_grad, head_grad, dq, do, du, dd = settle(*layer(
        tokens[0], norm_gain[None], head_gain, upstream[0],
        jnp.transpose(qkv_weight, (1, 0, 2)), out_weight, up_weight, down_weight,
    ))
    return (
        layer_out[None], token_grad[None], gain_grad[0], head_grad,
        jnp.transpose(dq, (1, 0, 2)), do, du, dd,
    )


def solution(mesh):
    placed = (
        P("dep", "in", "out"),
        P("out"),
        P(("out", "dep"), None, "in"),
        P(),
        P(("in", "dep"), "out"),
        P(("out", "dep"), "in"),
        P(("in", "dep"), "out"),
        P("dep", "in", "out"),
    )
    return jax.shard_map(
        body,
        mesh=mesh,
        in_specs=placed,
        out_specs=(
            P("dep", "in", "out"),
            P("dep", "in", "out"),
            P("out"),
            P(),
            P(("out", "dep"), None, "in"),
            P(("in", "dep"), "out"),
            P(("out", "dep"), "in"),
            P(("in", "dep"), "out"),
        ),
        check_vma=False,
    )
```

```python
import math

import jax
import jax.numpy as jnp
from jax import lax
from jax.experimental import pallas as pl
from jax.experimental.pallas import tpu as pltpu
from jax.sharding import PartitionSpec as P

MESH = pl.DeviceIdType.MESH
EPSILON = 1e-06
ROOT_HALF = 1.0 / math.sqrt(2.0)
ROOT_TWO_PI = math.sqrt(2.0 * math.pi)
SCALE = 128.0 ** (-0.5)
F32 = jnp.float32
BF16 = jnp.bfloat16
VMEM = pltpu.VMEM

TILES = (384, 384, 512, 512)
COLS = (1152, 384, 1536, 1536)
SHARD = ((96, 1152), (48, 768), (96, 1536), (192, 768))
SPLIT = (48, 32, 48, 96)
RING = (1, 7, 2, 6, 3, 5, 4)


def remote(src, dst, send, recv, device):
    return pltpu.make_async_remote_copy(
        src_ref=src, dst_ref=dst, send_sem=send, recv_sem=recv, device_id=device, device_id_type=MESH
    )


class Place:
    def __init__(self):
        self.i = lax.axis_index("in")
        self.o = lax.axis_index("out")
        self.d = lax.axis_index("dep")
        d = self.d
        x, y = d // 2, d % 2
        right, left, far = (x + 1) % 4, (x + 3) % 4, (x + 2) % 4
        self.me = d
        self.r, self.l, self.f = right * 2 + y, left * 2 + y, far * 2 + y
        self.p = x * 2 + 1 - y
        self.rp, self.lp, self.fp = right * 2 + 1 - y, left * 2 + 1 - y, far * 2 + 1 - y
        self.h, self.c = self.o // 2, self.o % 2
        self.mate = self.h * 2 + 1 - self.c
        self.cross = (1 - self.h) * 2 + self.c
        self.mate_at = {"out": self.mate}
        self.cross_at = {"out": self.cross, "dep": self.p}
        self.diag_at = {"out": (1 - self.h) * 2 + 1 - self.c, "dep": self.p}
        self.diag = (1 - self.h) * 2 + 1 - self.c
        self.table = (
            (self.r, self.l, self.me, self.l, "all"),
            (self.l, self.r, self.me, self.r, "all"),
            (self.p, self.p, self.me, self.p, "all"),
            (self.r, self.l, self.l, self.f, "low"),
            (self.l, self.r, self.r, self.f, "high"),
            (self.r, self.l, self.p, self.lp, "all"),
            (self.l, self.r, self.p, self.rp, "all"),
            (self.p, self.p, self.f, self.fp, "all"),
        )


def rows_of(slot, rows, split, part):
    start = slot * rows
    if part == "all":
        return pl.ds(pl.multiple_of(start, 16), rows)
    if part == "low":
        return pl.ds(pl.multiple_of(start, 16), split)
    return pl.ds(pl.multiple_of(start + split, 16), rows - split)


def greet(place):
    barrier = pltpu.get_barrier_semaphore()
    for k in range(1, 8):
        pl.semaphore_signal(barrier, inc=1, device_id={"in": (place.i + k) % 8}, device_id_type=MESH)
        pl.semaphore_signal(barrier, inc=1, device_id={"dep": (place.d + k) % 8}, device_id_type=MESH)
    for peer in (place.mate_at, place.cross_at, place.diag_at):
        pl.semaphore_signal(barrier, inc=1, device_id=peer, device_id_type=MESH)
    pl.semaphore_wait(barrier, 17)


def dot(a, b):
    return lax.dot_general(a, b, (((1,), (0,)), ((), ())), preferred_element_type=F32)


def dot_nt(a, b):
    return lax.dot_general(a, b, (((1,), (1,)), ((), ())), preferred_element_type=F32)


def dot_tn(a, b):
    return lax.dot_general(a, b, (((0,), (0,)), ((), ())), preferred_element_type=F32)


def normalize(values):
    average = jnp.mean(values, axis=-1, keepdims=True)
    spread = jnp.mean(values * values, axis=-1, keepdims=True) - average * average
    inverse = lax.rsqrt(spread + EPSILON)
    return ((values - average) * inverse, inverse)


def normalize_back(incoming, normed, inverse):
    first = jnp.mean(incoming, axis=-1, keepdims=True)
    second = jnp.mean(incoming * normed, axis=-1, keepdims=True)
    return inverse * (incoming - first - normed * second)


def layer_kernel(
    tokens, gain, head_gain, upstream, wq, wo, wu, wd,
    layer_out, token_grad, gain_grad, head_grad, dq, do, du, dd,
    gq, go, gu, gd, hid, grad, normed, inverse, fq, fo, fu, fd,
    stat_out, stat_in, away0, away1, away2, away3, home0, home1, home2, home3, in0, in1, in2, in3,
    xs_f, xs_q, xs_o, xs_u, xs_d, xr_f, xr_q, xr_o, xr_u, xr_d,
    kv, att, act, bg, qg, qlow, alow, hats, invs, kvpart, kvin, kvs, kvr,
    tok, ups, hid_t, lo_buf, lo_in, tg_buf, tg_in,
    pq, po, pu, pd, rq, ro, ru, rd, zsend0, zin0, zown0, ring_out, ring_in,
    tot_out, tot_in, vz_out, vz_in, vd_out, vd_in, hz_out, hz_in, hd_out, hd_in, ho_out, ho_in,
    gs, gr, gl, zs, zr, ss, sr, ms, mr, cs, cr, bs, br, ks, kr, ws, wr, vs, vr, es, er,
):
    place = Place()
    shards = (wq, wo, wu, wd)
    gathered = (gq, go, gu, gd)
    away, home, arrived, final = (away0, away1, away2, away3), (home0, home1, home2, home3), (in0, in1, in2, in3), (fq, fo, fu, fd)
    partial, returned, result = (pq, po, pu, pd), (rq, ro, ru, rd), (dq, do, du, dd)
    greet(place)
    pending = []

    def start(copy):
        copy.start()
        pending.append(copy)

    def local(src, dst, sem):
        copy = pltpu.make_async_copy(src, dst, sem)
        copy.start()
        return copy

    def slots(a, ref, rows):
        return ref.at[:, rows] if a == 0 else ref.at[rows]

    def gather_copy(a, k, receive=False):
        rows, _ = SHARD[a]
        target, _, mine, theirs, part = place.table[k]
        ref = slots(a, gathered[a], rows_of(theirs if receive else mine, rows, SPLIT[a], part))
        source = ref if receive or k > 2 else shards[a]
        return remote(source, ref, gs.at[a, k], gr.at[a, k], {"dep": target})

    def g_send(a, *kinds):
        for k in kinds:
            start(gather_copy(a, k))

    def g_wait(a, *kinds):
        for k in kinds:
            gather_copy(a, k, True).wait_recv()

    own_copies = [None] * 4

    def stage1(a):
        g_send(a, 0, 1, 2)
        rows, _ = SHARD[a]
        own_copies[a] = local(shards[a], slots(a, gathered[a], rows_of(place.me, rows, 0, "all")), gl.at[a])

    def stage2(a):
        g_wait(a, 0)
        g_send(a, 3)
        g_wait(a, 1)
        g_send(a, 4)
        g_wait(a, 2)
        g_send(a, 5, 6)

    def stage3(a):
        g_wait(a, 3, 4)
        g_send(a, 7)

    def stage4(a):
        g_wait(a, 5, 6, 7)
        own_copies[a].wait()

    def z_slot(ref, index):
        return ref.at[pl.ds(pl.multiple_of(index * 64, 64), 64)]

    def z_ring_copy(which, kind, ref, receive=False):
        turn = kind % 4
        if kind < 4:
            target, slot = (place.i + 1) % 8, (place.i + (7 if receive else 8) - turn) % 8
        else:
            target, slot = (place.i + 7) % 8, (place.i + (1 if receive else 0) + turn) % 8
        first = 32 if kind == 7 else 0
        at = ref.at[pl.ds(pl.multiple_of(slot * 64 + first, 32), 32 if turn == 3 else 64)]
        return remote(at, at, zs.at[which, kind], zr.at[which, kind], {"in": target})

    def z_round(which, ref, turn):
        for way in (0, 4):
            if turn > 0:
                z_ring_copy(which, way + turn - 1, ref, True).wait_recv()
            start(z_ring_copy(which, way + turn, ref))

    def z_done(which, ref):
        for way in (0, 4):
            z_ring_copy(which, way + 3, ref, True).wait_recv()

    def zsum_copy(which, k, send, recv):
        to = (place.i + k) % 8
        return remote(z_slot(send, to), recv.at[k - 1], zs.at[which, k - 1], zr.at[which, k - 1], {"in": to})

    def zsum_send(which, send, recv):
        for k in RING:
            start(zsum_copy(which, k, send, recv))

    def zsum_total(which, send, recv, mine):
        total = mine[...]
        for k in RING:
            zsum_copy(which, k, send, recv).wait_recv()
            total = total + recv[k - 1].astype(F32)
        return total

    def fan_copy(axis, index, size, k, send, recv, sem_s, sem_r):
        if axis == "out":
            peer = (place.mate_at, place.cross_at, place.diag_at)[k - 1]
        else:
            peer = {axis: (index + k) % size}
        return remote(send, recv.at[k - 1], sem_s.at[k - 1], sem_r.at[k - 1], peer)

    def fan_send(axis, index, size, send, recv, sem_s, sem_r):
        for k in range(1, size):
            start(fan_copy(axis, index, size, k, send, recv, sem_s, sem_r))

    def fan_total(axis, index, size, send, recv, sem_s, sem_r):
        total = send[...]
        for k in range(1, size):
            fan_copy(axis, index, size, k, send, recv, sem_s, sem_r).wait_recv()
            total = total + recv[k - 1]
        return total

    def out_rows(ref, index):
        return ref.at[pl.ds(pl.multiple_of(index * 128, 128), 128)]

    def out_copy(which, k, ref, receive=False):
        sent = (place.o, place.o, place.cross)[k]
        got = (place.mate, place.cross, place.diag)[k]
        target = (place.mate_at, place.cross_at, place.mate_at)[k]
        rows = out_rows(ref, got if receive else sent)
        return remote(rows, rows, bs.at[which, k], br.at[which, k], target)

    def out_send(which, ref):
        start(out_copy(which, 1, ref))
        start(out_copy(which, 0, ref))

    def out_relay(which, ref):
        out_copy(which, 1, ref, True).wait_recv()
        start(out_copy(which, 2, ref))

    def out_wait(which, ref):
        out_copy(which, 0, ref, True).wait_recv()
        out_copy(which, 2, ref, True).wait_recv()

    def swap_copy(k, source, landing):
        return remote(source, landing, es.at[k], er.at[k], {"dep": place.p})

    def swap_start(k, source, landing, result):
        @pl.when(place.h == 1)
        def _():
            swap_copy(k, source, landing).start()

        @pl.when(place.h == 0)
        def _():
            result[...] = source[...]

    def swap_end(k, source, landing, result):
        @pl.when(place.h == 1)
        def _():
            swap_copy(k, source, landing).wait()
            if result is not landing:
                result[...] = landing[...]

    swap_start(0, tokens, tok, tok)
    swap_start(1, upstream, ups, ups)
    stage1(0)
    stage1(1)
    swap_end(0, tokens, tok, tok)

    wide = tok[...].astype(F32)
    lane = lax.broadcasted_iota(jnp.int32, (64, 128), 1)
    total = jnp.sum(wide, axis=1, keepdims=True)
    square = jnp.sum(wide * wide, axis=1, keepdims=True)
    stat_out[...] = jnp.where(lane < 64, total, square)
    fan_send("out", place.o, 4, stat_out, stat_in, ss.at[0], sr.at[0])
    swap_end(1, upstream, ups, ups)
    z_slot(grad, place.i)[...] = ups[...]
    stats = fan_total("out", place.o, 4, stat_out, stat_in, ss.at[0], sr.at[0])
    average = stats[:, :1] * (1.0 / 3072.0)
    spread = stats[:, 64:65] * (1.0 / 3072.0) - average * average
    inv = lax.rsqrt(spread + EPSILON)
    norm = (wide - average) * inv
    normed[...] = norm
    inverse[...] = jnp.broadcast_to(inv, (64, 128))
    z_slot(hid, place.i)[...] = (norm * gain[...]).astype(BF16)
    z_round(0, hid, 0)
    z_round(1, grad, 0)
    stage2(0)
    z_round(0, hid, 1)
    stage2(1)
    stage1(2)
    z_round(0, hid, 2)
    stage3(0)
    z_round(0, hid, 3)
    z_round(1, grad, 1)
    stage3(1)

    def product(a, half, out):
        left = (hid if a in (0, 2) else grad)[pl.ds(pl.multiple_of(half * 256, 256), 256), :]
        tile = TILES[a]

        @pl.loop(0, COLS[a] // tile)
        def _(t):
            cols = pl.ds(pl.multiple_of(t * tile, 128), tile)
            if a == 0:
                out[:, cols] = dot(left, gathered[a][t])
            elif a == 2:
                out[:, cols] = dot(left, gathered[a][:, cols])
            else:
                out[:, cols] = dot_nt(left, gathered[a][cols, :])

    theirs = pl.ds(pl.multiple_of((1 - place.c) * 128, 128), 128)
    ours = pl.ds(pl.multiple_of(place.c * 128, 128), 128)

    def mate_copy(a, k):
        return remote(
            (away, home)[k][a].at[theirs], arrived[a].at[pl.ds(k * 128, 128)], ms.at[a, k], mr.at[a, k], place.mate_at
        )

    far_parts = (
        ((xs_f, xr_f, 0, 0, 768), (xs_q, xr_q, 1, 768, 384)),
        ((xs_o, xr_o, 2, 0, 384),),
        ((xs_u, xr_u, 3, 0, 1536),),
        ((xs_d, xr_d, 4, 0, 1536),),
    )

    def cross_copy(send, recv, k):
        return remote(send, recv, cs.at[k], cr.at[k], place.cross_at)

    def compute(a):
        product(a, 1 - place.h, away[a])
        mate_copy(a, 0).start()
        product(a, place.h, home[a])
        mate_copy(a, 1).start()
        mate_copy(a, 0).wait_recv()
        for send, recv, k, first, count in far_parts[a]:
            cols = slice(first, first + count)
            send[...] = (away[a][ours, cols] + arrived[a][:128, cols]).astype(send.dtype)
            start(cross_copy(send, recv, k))

    def reduce_far(a):
        mate_copy(a, 1).wait_recv()
        for send, recv, k, first, count in far_parts[a]:
            cols = slice(first, first + count)
            cross_copy(send, recv, k).wait_recv()
            final[a][:, cols] = home[a][ours, cols] + arrived[a][128:, cols] + recv[...].astype(F32)
        for k in range(2):
            mate_copy(a, k).wait_send()

    z_done(0, hid)
    stage4(0)
    compute(0)
    z_round(1, grad, 2)
    stage2(2)
    stage1(3)
    z_round(1, grad, 3)
    stage3(2)
    z_done(1, grad)
    stage4(1)
    compute(1)
    hid_t[...] = hid[...].T

    mine = pl.ds(pl.multiple_of(place.o * 128, 128), 128)
    reduce_far(0)
    for j in range(3):
        cols = slice(j * 128, (j + 1) * 128)
        for part in range(2):
            at = slice(part * 384 + j * 128, part * 384 + (j + 1) * 128)
            hat, hat_inv = normalize(fq[:, at])
            hats[:, at] = hat
            invs[:, at] = jnp.broadcast_to(hat_inv, (128, 128))
            low = (hat * head_gain[part : part + 1, :]).astype(BF16)
            if part == 0:
                qlow[:, cols] = low
            else:
                kv[mine, cols] = low
    kv[mine, 384:768] = fq[:, 768:1152].astype(BF16)
    out_send(0, kv)
    stage4(2)
    compute(2)
    out_relay(0, kv)
    reduce_far(1)
    alow[...] = fo[...].astype(BF16)
    stage2(3)
    out_wait(0, kv)

    def attend(j):
        cols = slice(j * 128, (j + 1) * 128)
        vals = slice(384 + j * 128, 384 + (j + 1) * 128)
        query, incoming = qlow[:, cols], alow[:, cols]
        keys, values = kv[:, cols], kv[:, vals]
        scores = dot_nt(query, keys) * SCALE
        raised = jnp.exp(scores - jnp.max(scores, axis=-1, keepdims=True))
        weights = raised / jnp.sum(raised, axis=-1, keepdims=True)
        weights_low = weights.astype(BF16)
        att[mine, cols] = dot(weights_low, values).astype(BF16)
        slopes = dot_nt(incoming, values)
        centre = jnp.sum(weights * slopes, axis=-1, keepdims=True)
        score_grad = (weights * (slopes - centre)).astype(BF16)
        kvpart[:, cols] = dot_tn(score_grad, query) * SCALE
        kvpart[:, vals] = dot_tn(weights_low, incoming)
        query_grad = dot(score_grad, keys) * SCALE
        hat = hats[:, cols]
        gain_part = jnp.sum(query_grad * hat, axis=0, keepdims=True)
        back = normalize_back(query_grad * head_gain[0:1, :], hat, invs[:, cols])
        qg[mine, cols] = back.astype(BF16)
        return gain_part

    def kv_near(h):
        rows = pl.ds(pl.multiple_of(h * 256 + (1 - place.c) * 128, 128), 128)
        return remote(kvpart.at[rows], kvin.at[h], ks.at[h], kr.at[h], place.mate_at)

    kv_far = remote(kvs, kvr, ks.at[2], kr.at[2], place.cross_at)
    def before_tile(t):
        cols = pl.ds(pl.multiple_of(t * 512, 512), 512)
        before = fu[:, cols]
        return cols, before, 0.5 * (1.0 + lax.erf(before * ROOT_HALF))

    query_gain = attend(0)
    stage3(3)
    query_gain = query_gain + attend(1)

    reduce_far(2)

    @pl.loop(0, 3)
    def _(t):
        cols, before, below = before_tile(t)
        act[mine, cols] = (before * below).astype(BF16)
        fu[:, cols] = below + before * jnp.exp(-0.5 * before * before) / ROOT_TWO_PI

    out_send(2, act)
    query_gain = query_gain + attend(2)
    for h in range(2):
        start(kv_near(h))
    out_send(1, att)
    for h in range(2):
        kv_near(h).wait_recv()
    other = pl.ds(pl.multiple_of(place.cross * 128, 128), 128)
    kvs[...] = (kvpart[other, :] + kvin[1 - place.h]).astype(kvs.dtype)
    start(kv_far)
    stage4(3)
    compute(3)
    def weight_product(a):
        tile = TILES[a]
        if a == 0:

            @pl.loop(0, 3)
            def _(t):
                pq[t] = dot(hid_t[...], qg[:, pl.ds(pl.multiple_of(t * tile, 128), tile)]).astype(BF16)
        elif a == 2:

            @pl.loop(0, 3)
            def _(t):
                cols = pl.ds(pl.multiple_of(t * tile, 128), tile)
                pu[:, cols] = dot(hid_t[...], bg[:, cols]).astype(BF16)
        else:
            left = att if a == 1 else act

            @pl.loop(0, COLS[a] // tile)
            def _(t):
                cols = pl.ds(pl.multiple_of(t * tile, 128), tile)
                partial[a][cols, :] = dot_tn(left[:, cols], grad[...]).astype(BF16)

    def back_place(a, k):
        rows, _ = SHARD[a]
        part = place.table[k][4]
        slot = (0, 1, 2, 3, 3, 4, 5, 6)[k]
        if part == "all":
            return returned[a].at[slot]
        if part == "low":
            return slots(a, returned[a].at[slot], pl.ds(0, SPLIT[a]))
        return slots(a, returned[a].at[slot], pl.ds(SPLIT[a], rows - SPLIT[a]))

    def back_copy(a, k):
        rows, _ = SHARD[a]
        _, target, _, slot, part = place.table[k]
        source = slots(a, partial[a], rows_of(slot, rows, SPLIT[a], part))
        return remote(source, back_place(a, k), ws.at[a, k], wr.at[a, k], {"dep": target})

    def b_send(a, *kinds):
        for k in kinds:
            start(back_copy(a, k))

    def b_add(a, *kinds):
        rows, _ = SHARD[a]
        for k in kinds:
            back_copy(a, k).wait_recv()
        _, _, slot, _, part = place.table[kinds[0]]
        at = slots(a, partial[a], rows_of(slot, rows, SPLIT[a], part))
        total = at[...].astype(F32)
        for k in kinds:
            total = total + back_place(a, k)[...].astype(F32)
        return at, total

    def b_merge(a, *kinds):
        at, total = b_add(a, *kinds)
        at[...] = total.astype(BF16)

    def back1(a):
        b_send(a, 7, 5, 6)

    def back2(a):
        b_merge(a, 7)
        b_send(a, 3, 4)
        b_merge(a, 5, 6)
        b_send(a, 2)

    def back3(a):
        b_merge(a, 3)
        b_send(a, 0)
        b_merge(a, 4)
        b_send(a, 1)

    def back4(a):
        _, total = b_add(a, 0, 1, 2)
        result[a][...] = total

    def to_in(which, send, recv, mine_ref, term):
        for b in range(2):
            rows = slice(b * 256, (b + 1) * 256)
            home0[:, :768] = term(rows)
            send[rows, :] = home0[:, :768].astype(BF16)

            @pl.when(place.i // 4 == b)
            def _():
                mine_ref[...] = home0[pl.ds(pl.multiple_of((place.i % 4) * 64, 64), 64), :768]

        zsum_send(which, send, recv)

    def block_of(index):
        index = index % 8
        rows = pl.ds(pl.multiple_of((index % 4) * 64, 64), 64)
        return away2.at[rows, pl.ds(pl.multiple_of((index // 4) * 768, 128), 768)]

    def ring_copy(way, step):
        target = (place.i + (1, 7)[way]) % 8
        rows = (pl.ds(0, 32), pl.ds(32, 32))[way] if step == 0 else pl.ds(0, 64)
        at = (way, step, rows)
        return remote(ring_out.at[at], ring_in.at[at], zs.at[3, way * 4 + step], zr.at[3, way * 4 + step], {"in": target})

    def ring_step(step):
        for way in range(2):
            block = block_of(place.i + (4 - step, 4 + step)[way])
            if step == 0:
                ring_out[way, 0] = block[...].astype(BF16)
            else:
                ring_copy(way, step - 1).wait_recv()
                if step == 1:
                    half = (slice(0, 32), slice(32, 64))[way]
                    block[half, :] += ring_in[way, 0, half, :].astype(F32)
                    ring_out[way, 1] = block[...].astype(BF16)
                else:
                    ring_out[way, step] = (block[...] + ring_in[way, step - 1].astype(F32)).astype(BF16)
            start(ring_copy(way, step))

    def ring_total():
        total = block_of(place.i)[...]
        for way in range(2):
            ring_copy(way, 3).wait_recv()
            total = total + ring_in[way, 3].astype(F32)
        return total

    out_relay(2, act)
    out_wait(2, act)
    weight_product(3)
    back1(3)
    out_relay(1, att)
    kv_far.wait_recv()
    key_gain = jnp.zeros((1, 128), F32)
    for j in range(3):
        cols = slice(j * 128, (j + 1) * 128)
        keys = slice(384 + j * 128, 384 + (j + 1) * 128)
        vals = slice(768 + j * 128, 768 + (j + 1) * 128)
        key_grad = kvpart[mine, cols] + kvin[place.h, :, cols] + kvr[:, cols].astype(F32)
        hat = hats[:, keys]
        key_gain = key_gain + jnp.sum(key_grad * hat, axis=0, keepdims=True)
        back = normalize_back(key_grad * head_gain[1:2, :], hat, invs[:, keys])
        qg[mine, keys] = back.astype(BF16)
        value_grad = kvpart[mine, keys] + kvin[place.h, :, keys] + kvr[:, keys].astype(F32)
        qg[mine, vals] = value_grad.astype(BF16)
    out_send(4, qg)
    row = lax.broadcasted_iota(jnp.int32, (8, 128), 0)
    hz_out[...] = jnp.where(row == 0, query_gain, jnp.where(row == 1, key_gain, 0.0))
    fan_send("in", place.i, 8, hz_out, hz_in, vs.at[0], vr.at[0])

    out_wait(1, att)
    weight_product(1)
    back1(1)
    back2(3)
    to_in(2, zsend0, zin0, zown0, lambda r: dot(att[r, :], go[...]) + dot(act[r, :], gd[...]))
    reduce_far(3)

    @pl.loop(0, 3)
    def _(t):
        cols = pl.ds(pl.multiple_of(t * 512, 512), 512)
        bg[mine, cols] = (fd[:, cols] * fu[:, cols]).astype(BF16)

    out_send(3, bg)
    back2(1)
    out_relay(4, qg)
    out_wait(4, qg)
    weight_product(0)
    back1(0)
    back3(3)
    for b in range(2):
        rows = slice(b * 256, (b + 1) * 256)
        away2[:, b * 768 : (b + 1) * 768] = sum(
            dot_nt(qg[rows, part * 384 : (part + 1) * 384], gq[part]) for part in range(3)
        )
    back2(0)
    out_relay(3, bg)
    out_wait(3, bg)
    weight_product(2)
    back1(2)
    for b in range(2):
        rows = slice(b * 256, (b + 1) * 256)
        away2[:, b * 768 : (b + 1) * 768] += dot_nt(bg[rows, :], gu[...])
    ring_step(0)
    back3(1)
    back3(0)
    ring_step(1)
    back2(2)
    ring_step(2)
    hd_out[...] = fan_total("in", place.i, 8, hz_out, hz_in, vs.at[0], vr.at[0])
    fan_send("dep", place.d, 8, hd_out, hd_in, vs.at[1], vr.at[1])
    lo_buf[...] = (tok[...].astype(F32) + zsum_total(2, zsend0, zin0, zown0)).astype(BF16)
    swap_start(2, lo_buf, lo_in, layer_out)
    ring_step(3)
    back3(2)

    input_grad = ring_total()
    scaled = input_grad * gain[...]
    first = jnp.sum(scaled, axis=1, keepdims=True)
    second = jnp.sum(scaled * normed[...], axis=1, keepdims=True)
    tot_out[...] = jnp.where(lane < 64, first, second)
    fan_send("out", place.o, 4, tot_out, tot_in, ss.at[1], sr.at[1])
    vz_out[...] = jnp.sum(input_grad * normed[...], axis=0, keepdims=True)
    fan_send("in", place.i, 8, vz_out, vz_in, vs.at[2], vr.at[2])
    back4(1)
    back4(3)
    totals = fan_total("out", place.o, 4, tot_out, tot_in, ss.at[1], sr.at[1])
    centred = scaled - totals[:, :1] * (1.0 / 3072.0) - normed[...] * (totals[:, 64:65] * (1.0 / 3072.0))
    tg_buf[...] = (ups[...].astype(F32) + inverse[:, :1] * centred).astype(BF16)
    swap_start(3, tg_buf, tg_in, token_grad)
    vd_out[...] = fan_total("in", place.i, 8, vz_out, vz_in, vs.at[2], vr.at[2])
    fan_send("dep", place.d, 8, vd_out, vd_in, vs.at[3], vr.at[3])
    ho_out[...] = fan_total("dep", place.d, 8, hd_out, hd_in, vs.at[1], vr.at[1])
    fan_send("out", place.o, 4, ho_out, ho_in, ss.at[2], sr.at[2])
    back4(0)
    back4(2)
    head_grad[...] = fan_total("out", place.o, 4, ho_out, ho_in, ss.at[2], sr.at[2])[:2]
    swap_end(2, lo_buf, lo_in, layer_out)
    swap_end(3, tg_buf, tg_in, token_grad)
    gain_grad[...] = fan_total("dep", place.d, 8, vd_out, vd_in, vs.at[3], vr.at[3])
    for copy in pending:
        copy.wait_send()


def layer(tokens, gain, head_gain, upstream, wq, wo, wu, wd):
    shape = jax.ShapeDtypeStruct
    outs = [
        shape((64, 768), BF16), shape((64, 768), BF16), shape((1, 768), F32), shape((2, 128), F32),
        shape((3, 96, 384), F32), shape((48, 768), F32), shape((96, 1536), F32), shape((192, 768), F32),
    ]
    whole = pl.BlockSpec(memory_space=VMEM)
    far = [VMEM((128, 768), F32), VMEM((128, 384), BF16), VMEM((128, 384), BF16), VMEM((128, 1536), BF16), VMEM((128, 1536), BF16)]
    full = [VMEM((3, 768, 384), BF16), VMEM((384, 768), BF16), VMEM((768, 1536), BF16), VMEM((1536, 768), BF16)]
    scratch = full + [VMEM((512, 768), BF16), VMEM((512, 768), BF16), VMEM((64, 768), F32), VMEM((64, 128), F32)]
    scratch += [VMEM((128, n), F32) for n in COLS]
    scratch += [VMEM((64, 128), F32), VMEM((3, 64, 128), F32)]
    for _ in range(3):
        scratch += [VMEM((256, n), F32) for n in COLS]
    scratch += far + far
    scratch += [VMEM((512, n), BF16) for n in (768, 384, 1536, 1536, 1152)]
    scratch += [VMEM((128, 384), BF16), VMEM((128, 384), BF16), VMEM((128, 768), F32), VMEM((128, 768), F32)]
    scratch += [VMEM((512, 768), F32), VMEM((2, 128, 768), F32), VMEM((128, 768), BF16), VMEM((128, 768), BF16)]
    scratch += [VMEM((64, 768), BF16)] * 2 + [VMEM((768, 512), BF16)] + [VMEM((64, 768), BF16)] * 4
    scratch += full + [VMEM((7, 3, 96, 384), BF16)] + [VMEM((7, rows, cols), BF16) for rows, cols in SHARD[1:]]
    scratch += [VMEM((512, 768), BF16), VMEM((7, 64, 768), BF16), VMEM((64, 768), F32)] + [VMEM((2, 4, 64, 768), BF16)] * 2
    scratch += [VMEM((64, 128), F32), VMEM((3, 64, 128), F32)]
    scratch += [VMEM((1, 768), F32), VMEM((7, 1, 768), F32)] * 2
    scratch += [VMEM((8, 128), F32), VMEM((7, 8, 128), F32)] * 2
    scratch += [VMEM((8, 128), F32), VMEM((3, 8, 128), F32)]
    dma = pltpu.SemaphoreType.DMA
    scratch += [dma((4, 8)), dma((4, 8)), dma((4,)), dma((4, 8)), dma((4, 8)), dma((3, 3)), dma((3, 3))]
    scratch += [dma((4, 2)), dma((4, 2)), dma((5,)), dma((5,)), dma((5, 3)), dma((5, 3)), dma((3,)), dma((3,))]
    scratch += [dma((4, 8)), dma((4, 8)), dma((4, 7)), dma((4, 7)), dma((4,)), dma((4,))]
    return pl.pallas_call(
        layer_kernel,
        out_shape=outs,
        in_specs=[whole] * 4 + [pl.BlockSpec(memory_space=pl.ANY)] * 4,
        out_specs=[whole] * len(outs),
        scratch_shapes=scratch,
        compiler_params=pltpu.CompilerParams(collective_id=1, has_side_effects=True, vmem_limit_bytes=62 * 2**20),
        cost_estimate=pl.CostEstimate(flops=11 * 10**9, bytes_accessed=10**7, transcendentals=10**6),
    )(tokens, gain, head_gain, upstream, wq, wo, wu, wd)


def settle_kernel(*refs):
    sources, targets, stages, sems = refs[:8], refs[8:16], refs[16:24], refs[24]
    loads = [pltpu.make_async_copy(a, b, sems.at[0, k]) for k, (a, b) in enumerate(zip(sources, stages))]
    stores = [pltpu.make_async_copy(a, b, sems.at[1, k]) for k, (a, b) in enumerate(zip(stages, targets))]
    for copy in loads:
        copy.start()
    for load, store in zip(loads, stores):
        load.wait()
        store.start()
    for copy in stores:
        copy.wait()


def settle(*arrays):
    anywhere = pl.BlockSpec(memory_space=pl.ANY)
    return pl.pallas_call(
        settle_kernel,
        out_shape=[jax.ShapeDtypeStruct(a.shape, a.dtype) for a in arrays],
        in_specs=[anywhere] * 8,
        out_specs=[anywhere] * 8,
        scratch_shapes=[VMEM(a.shape, a.dtype) for a in arrays] + [pltpu.SemaphoreType.DMA((2, 8))],
        compiler_params=pltpu.CompilerParams(vmem_limit_bytes=60 * 2**20),
        cost_estimate=pl.CostEstimate(flops=0, bytes_accessed=8 * 10**6, transcendentals=0),
    )(*arrays)


def body(tokens, norm_gain, qkv_weight, head_gain, out_weight, up_weight, down_weight, upstream):
    layer_out, token_grad, gain_grad, head_grad, dq, do, du, dd = settle(*layer(
        tokens[0], norm_gain[None], head_gain, upstream[0],
        jnp.transpose(qkv_weight, (1, 0, 2)), out_weight, up_weight, down_weight,
    ))
    return (
        layer_out[None], token_grad[None], gain_grad[0], head_grad,
        jnp.transpose(dq, (1, 0, 2)), do, du, dd,
    )


def solution(mesh):
    placed = (
        P("dep", "in", "out"),
        P("out"),
        P(("out", "dep"), None, "in"),
        P(),
        P(("in", "dep"), "out"),
        P(("out", "dep"), "in"),
        P(("in", "dep"), "out"),
        P("dep", "in", "out"),
    )
    return jax.shard_map(
        body,
        mesh=mesh,
        in_specs=placed,
        out_specs=(
            P("dep", "in", "out"),
            P("dep", "in", "out"),
            P("out"),
            P(),
            P(("out", "dep"), None, "in"),
            P(("in", "dep"), "out"),
            P(("out", "dep"), "in"),
            P(("in", "dep"), "out"),
        ),
        check_vma=False,
    )
```

```python
import math

import jax
import jax.numpy as jnp
from jax import lax
from jax.experimental import pallas as pl
from jax.experimental.pallas import tpu as pltpu
from jax.sharding import PartitionSpec as P

MESH = pl.DeviceIdType.MESH
EPSILON = 1e-06
ROOT_HALF = 1.0 / math.sqrt(2.0)
ROOT_TWO_PI = math.sqrt(2.0 * math.pi)
SCALE = 128.0 ** (-0.5)
F32 = jnp.float32
BF16 = jnp.bfloat16
VMEM = pltpu.VMEM

TILES = (384, 384, 512, 512)
COLS = (1152, 384, 1536, 1536)
SHARD = ((96, 1152), (48, 768), (96, 1536), (192, 768))
SPLIT = (48, 32, 48, 96)
BACK_ROWS = (96, 48, 96, 192, 96)
BACK_SPLIT = (48, 32, 48, 96, 48)
RING = (1, 7, 2, 6, 3, 5, 4)


def remote(src, dst, send, recv, device):
    return pltpu.make_async_remote_copy(
        src_ref=src, dst_ref=dst, send_sem=send, recv_sem=recv, device_id=device, device_id_type=MESH
    )


class Place:
    def __init__(self):
        self.i = lax.axis_index("in")
        self.o = lax.axis_index("out")
        self.d = lax.axis_index("dep")
        d = self.d
        x, y = d // 2, d % 2
        right, left, far = (x + 1) % 4, (x + 3) % 4, (x + 2) % 4
        self.me = d
        self.r, self.l, self.f = right * 2 + y, left * 2 + y, far * 2 + y
        self.p = x * 2 + 1 - y
        self.rp, self.lp, self.fp = right * 2 + 1 - y, left * 2 + 1 - y, far * 2 + 1 - y
        self.h, self.c = self.o // 2, self.o % 2
        self.mate = self.h * 2 + 1 - self.c
        self.cross = (1 - self.h) * 2 + self.c
        self.mate_at = {"out": self.mate}
        self.cross_at = {"out": self.cross, "dep": self.p}
        self.diag_at = {"out": (1 - self.h) * 2 + 1 - self.c, "dep": self.p}
        self.diag = (1 - self.h) * 2 + 1 - self.c
        self.table = (
            (self.r, self.l, self.me, self.l, "all"),
            (self.l, self.r, self.me, self.r, "all"),
            (self.p, self.p, self.me, self.p, "all"),
            (self.r, self.l, self.l, self.f, "low"),
            (self.l, self.r, self.r, self.f, "high"),
            (self.r, self.l, self.p, self.lp, "all"),
            (self.l, self.r, self.p, self.rp, "all"),
            (self.p, self.p, self.f, self.fp, "all"),
        )


def rows_of(slot, rows, split, part):
    start = slot * rows
    if part == "all":
        return pl.ds(pl.multiple_of(start, 16), rows)
    if part == "low":
        return pl.ds(pl.multiple_of(start, 16), split)
    return pl.ds(pl.multiple_of(start + split, 16), rows - split)


def greet(place):
    barrier = pltpu.get_barrier_semaphore()
    for k in range(1, 8):
        pl.semaphore_signal(barrier, inc=1, device_id={"in": (place.i + k) % 8}, device_id_type=MESH)
        pl.semaphore_signal(barrier, inc=1, device_id={"dep": (place.d + k) % 8}, device_id_type=MESH)
    for peer in (place.mate_at, place.cross_at, place.diag_at):
        pl.semaphore_signal(barrier, inc=1, device_id=peer, device_id_type=MESH)
    pl.semaphore_wait(barrier, 17)


def dot(a, b):
    return lax.dot_general(a, b, (((1,), (0,)), ((), ())), preferred_element_type=F32)


def dot_nt(a, b):
    return lax.dot_general(a, b, (((1,), (1,)), ((), ())), preferred_element_type=F32)


def dot_tn(a, b):
    return lax.dot_general(a, b, (((0,), (0,)), ((), ())), preferred_element_type=F32)


def normalize(values):
    average = jnp.mean(values, axis=-1, keepdims=True)
    spread = jnp.mean(values * values, axis=-1, keepdims=True) - average * average
    inverse = lax.rsqrt(spread + EPSILON)
    return ((values - average) * inverse, inverse)


def normalize_back(incoming, normed, inverse):
    first = jnp.mean(incoming, axis=-1, keepdims=True)
    second = jnp.mean(incoming * normed, axis=-1, keepdims=True)
    return inverse * (incoming - first - normed * second)


def layer_kernel(
    tokens, gain, head_gain, upstream, wq, wo, wu, wd,
    layer_out, token_grad, gain_grad, head_grad, dq, do, du, dd,
    gq, go, gu, gd, hid, grad, normed, inverse, fq, fo, fu,
    stat_out, stat_in, away0, away1, away2, away3, home0, home1, home2, home3, in0, in1, in2, in3,
    xs_f, xs_q, xs_o, xs_u, xs_d, xs_e, xr_f, xr_q, xr_o, xr_u, xr_d, xr_e,
    kv, att, act, bg0, bg1, qg, qlow, alow, hats, invs, kvpart, kvin, kvs, kvr,
    tok, ups, hid_t, lo_buf, lo_in, tg_buf, tg_in,
    pq, po, pu, pd, pv, rq, ro, ru, rd, rv, ring_out, ring_in,
    tot_out, tot_in, vz_out, vz_in, vd_out, vd_in, hz_out, hz_in, hd_out, hd_in, ho_out, ho_in,
    gs, gr, gl, zs, zr, ss, sr, ms, mr, cs, cr, bs, br, ks, kr, ws, wr, vs, vr, es, er,
):
    place = Place()
    bg = (bg0, bg1)
    shards = (wq, wo, wu, wd)
    gathered = (gq, go, gu, gd)
    away, home, arrived, final = (away0, away1, away2, away3), (home0, home1, home2, home3), (in0, in1, in2, in3), (fq, fo, fu)
    partial, returned = (pq, po, pu, pd, pv), (rq, ro, ru, rd, rv)
    result = (dq, do, du.at[:, :768], dd, du.at[:, 768:])
    greet(place)
    pending = []

    def start(copy):
        copy.start()
        pending.append(copy)

    def local(src, dst, sem):
        copy = pltpu.make_async_copy(src, dst, sem)
        copy.start()
        return copy

    def slots(a, ref, rows):
        return ref.at[:, rows] if a == 0 else ref.at[rows]

    def gather_copy(a, k, receive=False):
        rows, _ = SHARD[a]
        target, _, mine, theirs, part = place.table[k]
        ref = slots(a, gathered[a], rows_of(theirs if receive else mine, rows, SPLIT[a], part))
        source = ref if receive or k > 2 else shards[a]
        return remote(source, ref, gs.at[a, k], gr.at[a, k], {"dep": target})

    def g_send(a, *kinds):
        for k in kinds:
            start(gather_copy(a, k))

    def g_wait(a, *kinds):
        for k in kinds:
            gather_copy(a, k, True).wait_recv()

    own_copies = [None] * 4

    def stage1(a):
        g_send(a, 0, 1, 2)
        rows, _ = SHARD[a]
        own_copies[a] = local(shards[a], slots(a, gathered[a], rows_of(place.me, rows, 0, "all")), gl.at[a])

    def pass_left(a):
        g_wait(a, 0)
        g_send(a, 3)

    def pass_right(a):
        g_wait(a, 1)
        g_send(a, 4)

    def pass_pair(a):
        g_wait(a, 2)
        g_send(a, 5, 6)

    def stage3(a):
        g_wait(a, 3, 4)
        g_send(a, 7)

    def stage4(a):
        g_wait(a, 5, 6, 7)
        own_copies[a].wait()

    def z_slot(ref, index):
        return ref.at[pl.ds(pl.multiple_of(index * 64, 64), 64)]

    def z_ring_copy(which, kind, ref, receive=False):
        turn = kind % 4
        if kind < 4:
            target, slot = (place.i + 1) % 8, (place.i + (7 if receive else 8) - turn) % 8
        else:
            target, slot = (place.i + 7) % 8, (place.i + (1 if receive else 0) + turn) % 8
        first = 32 if kind == 7 else 0
        at = ref.at[pl.ds(pl.multiple_of(slot * 64 + first, 32), 32 if turn == 3 else 64)]
        return remote(at, at, zs.at[which, kind], zr.at[which, kind], {"in": target})

    def z_round(which, ref, turn):
        for way in (0, 4):
            if turn > 0:
                z_ring_copy(which, way + turn - 1, ref, True).wait_recv()
            start(z_ring_copy(which, way + turn, ref))

    complete = set()

    def z_done(which, ref):
        if ("z", which) not in complete:
            complete.add(("z", which))
            for way in (0, 4):
                z_ring_copy(which, way + 3, ref, True).wait_recv()

    def fan_copy(axis, index, size, k, send, recv, sem_s, sem_r):
        if axis == "out":
            peer = (place.mate_at, place.cross_at, place.diag_at)[k - 1]
        else:
            peer = {axis: (index + k) % size}
        return remote(send, recv.at[k - 1], sem_s.at[k - 1], sem_r.at[k - 1], peer)

    def fan_send(axis, index, size, send, recv, sem_s, sem_r):
        for k in range(1, size):
            start(fan_copy(axis, index, size, k, send, recv, sem_s, sem_r))

    def fan_total(axis, index, size, send, recv, sem_s, sem_r):
        total = send[...]
        for k in range(1, size):
            fan_copy(axis, index, size, k, send, recv, sem_s, sem_r).wait_recv()
            total = total + recv[k - 1]
        return total

    def out_rows(ref, index):
        return ref.at[pl.ds(pl.multiple_of(index * 128, 128), 128)]

    def out_copy(which, k, ref, receive=False):
        sent = (place.o, place.o, place.cross)[k]
        got = (place.mate, place.cross, place.diag)[k]
        target = (place.mate_at, place.cross_at, place.mate_at)[k]
        rows = out_rows(ref, got if receive else sent)
        return remote(rows, rows, bs.at[which, k], br.at[which, k], target)

    def out_send(which, ref):
        start(out_copy(which, 1, ref))
        start(out_copy(which, 0, ref))

    def out_relay(which, ref):
        out_copy(which, 1, ref, True).wait_recv()
        start(out_copy(which, 2, ref))

    def out_wait(which, ref):
        if ("out", which) not in complete:
            complete.add(("out", which))
            out_copy(which, 0, ref, True).wait_recv()
            out_copy(which, 2, ref, True).wait_recv()

    def swap_copy(k, source, landing):
        return remote(source, landing, es.at[k], er.at[k], {"dep": place.p})

    def swap_start(k, source, landing, result):
        @pl.when(place.h == 1)
        def _():
            swap_copy(k, source, landing).start()

        @pl.when(place.h == 0)
        def _():
            result[...] = source[...]

    def swap_end(k, source, landing, result):
        @pl.when(place.h == 1)
        def _():
            swap_copy(k, source, landing).wait()
            if result is not landing:
                result[...] = landing[...]

    swap_start(0, tokens, tok, tok)
    swap_start(1, upstream, ups, ups)
    lane = lax.broadcasted_iota(jnp.int32, (64, 128), 1)

    def statistics():
        swap_end(0, tokens, tok, tok)
        wide = tok[...].astype(F32)
        total = jnp.sum(wide, axis=1, keepdims=True)
        square = jnp.sum(wide * wide, axis=1, keepdims=True)
        stat_out[...] = jnp.where(lane < 64, total, square)
        fan_send("out", place.o, 4, stat_out, stat_in, ss.at[0], sr.at[0])
        swap_end(1, upstream, ups, ups)
        z_slot(grad, place.i)[...] = ups[...]
        stats = fan_total("out", place.o, 4, stat_out, stat_in, ss.at[0], sr.at[0])
        average = stats[:, :1] * (1.0 / 3072.0)
        spread = stats[:, 64:65] * (1.0 / 3072.0) - average * average
        inv = lax.rsqrt(spread + EPSILON)
        norm = (wide - average) * inv
        normed[...] = norm
        inverse[...] = jnp.broadcast_to(inv, (64, 128))
        z_slot(hid, place.i)[...] = (norm * gain[...]).astype(BF16)

    def product(a, half, out):
        left = (hid if a in (0, 2) else grad)[pl.ds(pl.multiple_of(half * 256, 256), 256), :]
        tile = TILES[a]

        @pl.loop(0, COLS[a] // tile)
        def _(t):
            cols = pl.ds(pl.multiple_of(t * tile, 128), tile)
            if a == 0:
                out[:, cols] = dot(left, gathered[a][t])
            elif a == 2:
                out[:, cols] = dot(left, gathered[a][:, cols])
            else:
                out[:, cols] = dot_nt(left, gathered[a][cols, :])

    theirs = pl.ds(pl.multiple_of((1 - place.c) * 128, 128), 128)
    ours = pl.ds(pl.multiple_of(place.c * 128, 128), 128)

    def mate_copy(a, k):
        return remote(
            (away, home)[k][a].at[theirs], arrived[a].at[pl.ds(k * 128, 128)], ms.at[a, k], mr.at[a, k], place.mate_at
        )

    far_parts = (
        ((xs_f, xr_f, 0, 0, 768), (xs_q, xr_q, 1, 768, 384)),
        ((xs_o, xr_o, 2, 0, 384),),
        ((xs_u, xr_u, 3, 0, 1536),),
        ((xs_d, xr_d, 4, 0, 768), (xs_e, xr_e, 5, 768, 768)),
    )

    def cross_copy(send, recv, k):
        return remote(send, recv, cs.at[k], cr.at[k], place.cross_at)

    def depart(a):
        stage4(a)
        z_done(*((0, hid) if a in (0, 2) else (1, grad)))
        product(a, 1 - place.h, away[a])
        mate_copy(a, 0).start()

    def remain(a):
        product(a, place.h, home[a])
        mate_copy(a, 1).start()

    def reduce_near(a):
        mate_copy(a, 0).wait_recv()
        for send, recv, k, first, count in far_parts[a]:
            cols = slice(first, first + count)
            send[...] = (away[a][ours, cols] + arrived[a][:128, cols]).astype(send.dtype)
            start(cross_copy(send, recv, k))

    def home_wait(a):
        if ("home", a) not in complete:
            complete.add(("home", a))
            mate_copy(a, 1).wait_recv()
            for k in range(2):
                mate_copy(a, k).wait_send()

    def far_sum(a, part):
        send, recv, k, first, count = far_parts[a][part]
        cols = slice(first, first + count)
        cross_copy(send, recv, k).wait_recv()
        return cols, home[a][ours, cols] + arrived[a][128:, cols] + recv[...].astype(F32)

    def reduce_far(a):
        home_wait(a)
        for part in range(len(far_parts[a])):
            cols, total = far_sum(a, part)
            final[a][:, cols] = total

    def transpose_hidden():
        z_done(0, hid)
        hid_t[...] = hid[...].T

    mine = pl.ds(pl.multiple_of(place.o * 128, 128), 128)

    def heads():
        for j in range(3):
            cols = slice(j * 128, (j + 1) * 128)
            for part in range(2):
                at = slice(part * 384 + j * 128, part * 384 + (j + 1) * 128)
                hat, hat_inv = normalize(fq[:, at])
                hats[:, at] = hat
                invs[:, at] = jnp.broadcast_to(hat_inv, (128, 128))
                low = (hat * head_gain[part : part + 1, :]).astype(BF16)
                if part == 0:
                    qlow[:, cols] = low
                else:
                    kv[mine, cols] = low
        kv[mine, 384:768] = fq[:, 768:1152].astype(BF16)
        out_send(0, kv)

    gains = []

    def attend(j):
        if j == 0:
            out_wait(0, kv)
            alow[...] = fo[...].astype(BF16)
        cols = slice(j * 128, (j + 1) * 128)
        vals = slice(384 + j * 128, 384 + (j + 1) * 128)
        query, incoming = qlow[:, cols], alow[:, cols]
        keys, values = kv[:, cols], kv[:, vals]
        scores = dot_nt(query, keys) * SCALE
        raised = jnp.exp(scores - jnp.max(scores, axis=-1, keepdims=True))
        weights = raised / jnp.sum(raised, axis=-1, keepdims=True)
        weights_low = weights.astype(BF16)
        att[mine, cols] = dot(weights_low, values).astype(BF16)
        slopes = dot_nt(incoming, values)
        centre = jnp.sum(weights * slopes, axis=-1, keepdims=True)
        score_grad = (weights * (slopes - centre)).astype(BF16)
        kvpart[:, cols] = dot_tn(score_grad, query) * SCALE
        kvpart[:, vals] = dot_tn(weights_low, incoming)
        query_grad = dot(score_grad, keys) * SCALE
        hat = hats[:, cols]
        gain_part = jnp.sum(query_grad * hat, axis=0, keepdims=True)
        back = normalize_back(query_grad * head_gain[0:1, :], hat, invs[:, cols])
        qg[mine, cols] = back.astype(BF16)
        gains.append(gain_part)

    def kv_near(h):
        rows = pl.ds(pl.multiple_of(h * 256 + (1 - place.c) * 128, 128), 128)
        return remote(kvpart.at[rows], kvin.at[h], ks.at[h], kr.at[h], place.mate_at)

    kv_far = remote(kvs, kvr, ks.at[2], kr.at[2], place.cross_at)
    def before_tile(t):
        cols = pl.ds(pl.multiple_of(t * 512, 512), 512)
        before = fu[:, cols]
        return cols, before, 0.5 * (1.0 + lax.erf(before * ROOT_HALF))

    def attend_send():
        for h in range(2):
            start(kv_near(h))
        out_send(1, att)

    def kv_across():
        for h in range(2):
            kv_near(h).wait_recv()
        other = pl.ds(pl.multiple_of(place.cross * 128, 128), 128)
        kvs[...] = (kvpart[other, :] + kvin[1 - place.h]).astype(kvs.dtype)
        start(kv_far)

    def activate():
        @pl.loop(0, 3)
        def _(t):
            cols, before, below = before_tile(t)
            act[mine, cols] = (before * below).astype(BF16)
            fu[:, cols] = below + before * jnp.exp(-0.5 * before * before) / ROOT_TWO_PI

        out_send(2, act)

    def before_back(part):
        home_wait(3)
        cols, total = far_sum(3, part)
        bg[part][mine, :] = (total * fu[:, cols]).astype(BF16)
        out_send((3, 5)[part], bg[part])

    def keys_back():
        kv_far.wait_recv()
        key_gain = jnp.zeros((1, 128), F32)
        for j in range(3):
            cols = slice(j * 128, (j + 1) * 128)
            keys = slice(384 + j * 128, 384 + (j + 1) * 128)
            vals = slice(768 + j * 128, 768 + (j + 1) * 128)
            key_grad = kvpart[mine, cols] + kvin[place.h, :, cols] + kvr[:, cols].astype(F32)
            hat = hats[:, keys]
            key_gain = key_gain + jnp.sum(key_grad * hat, axis=0, keepdims=True)
            back = normalize_back(key_grad * head_gain[1:2, :], hat, invs[:, keys])
            qg[mine, keys] = back.astype(BF16)
            value_grad = kvpart[mine, keys] + kvin[place.h, :, keys] + kvr[:, keys].astype(F32)
            qg[mine, vals] = value_grad.astype(BF16)
        out_send(4, qg)
        row = lax.broadcasted_iota(jnp.int32, (8, 128), 0)
        query_gain = gains[0] + gains[1] + gains[2]
        hz_out[...] = jnp.where(row == 0, query_gain, jnp.where(row == 1, key_gain, 0.0))
        fan_send("in", place.i, 8, hz_out, hz_in, vs.at[0], vr.at[0])

    def down_product(turn):
        if turn == 0:
            out_wait(2, act)
            z_done(1, grad)
        slot = (place.f, place.l, place.r, place.me)[turn]
        cols = pl.ds(pl.multiple_of((slot // 2) * 384, 128), 384)
        pd[cols, :] = dot_tn(act[:, cols], grad[...]).astype(BF16)
        if turn < 3:
            b_send(3, (7, 5, 6)[turn])

    def weight_product(a):
        if a == 0:
            out_wait(4, qg)

            @pl.loop(0, 3)
            def _(t):
                pq[t] = dot(hid_t[...], qg[:, pl.ds(pl.multiple_of(t * 384, 128), 384)]).astype(BF16)
        elif a == 1:
            out_wait(1, att)
            po[...] = dot_tn(att[...], grad[...]).astype(BF16)
        else:
            which, right, target = (3, bg[0], pu) if a == 2 else (5, bg[1], pv)
            out_wait(which, right)

            @pl.loop(0, 2)
            def _(t):
                cols = pl.ds(pl.multiple_of(t * 384, 128), 384)
                target[:, cols] = dot(hid_t[...], right[:, cols]).astype(BF16)

        b_send(a, 7, 5, 6)

    def back_place(a, k):
        rows = BACK_ROWS[a]
        part = place.table[k][4]
        slot = (0, 1, 2, 3, 3, 4, 5, 6)[k]
        if part == "all":
            return returned[a].at[slot]
        if part == "low":
            return slots(a, returned[a].at[slot], pl.ds(0, BACK_SPLIT[a]))
        return slots(a, returned[a].at[slot], pl.ds(BACK_SPLIT[a], rows - BACK_SPLIT[a]))

    def back_copy(a, k):
        rows = BACK_ROWS[a]
        _, target, _, slot, part = place.table[k]
        source = slots(a, partial[a], rows_of(slot, rows, BACK_SPLIT[a], part))
        return remote(source, back_place(a, k), ws.at[a, k], wr.at[a, k], {"dep": target})

    def b_send(a, *kinds):
        for k in kinds:
            start(back_copy(a, k))

    def b_add(a, *kinds):
        rows = BACK_ROWS[a]
        for k in kinds:
            back_copy(a, k).wait_recv()
        _, _, slot, _, part = place.table[kinds[0]]
        at = slots(a, partial[a], rows_of(slot, rows, BACK_SPLIT[a], part))
        total = at[...].astype(F32)
        for k in kinds:
            total = total + back_place(a, k)[...].astype(F32)
        return at, total

    def b_merge(a, *kinds):
        at, total = b_add(a, *kinds)
        at[...] = total.astype(BF16)

    def back_far(a):
        b_merge(a, 7)
        b_send(a, 3, 4)

    def back_pair(a):
        b_merge(a, 5, 6)
        b_send(a, 2)

    def back_left(a):
        b_merge(a, 3)
        b_send(a, 0)

    def back_right(a):
        b_merge(a, 4)
        b_send(a, 1)

    def back4(a):
        _, total = b_add(a, 0, 1, 2)
        result[a][...] = total

    totals_of = (home2, away2)

    def block_of(which, index):
        index = index % 8
        rows = pl.ds(pl.multiple_of((index % 4) * 64, 64), 64)
        return totals_of[which].at[rows, pl.ds(pl.multiple_of((index // 4) * 768, 128), 768)]

    def add_terms(which, term):
        for b in range(2):
            rows, cols = slice(b * 256, (b + 1) * 256), slice(b * 768, (b + 1) * 768)
            value = term(rows)
            if which in complete:
                value = totals_of[which][:, cols] + value
            totals_of[which][:, cols] = value
        complete.add(which)

    def mix():
        out_wait(1, att)
        out_wait(2, act)
        add_terms(0, lambda r: dot(att[r, :], go[...]) + dot(act[r, :], gd[...]))

    def input_heads():
        out_wait(4, qg)
        add_terms(1, lambda r: sum(dot_nt(qg[r, k * 384 : (k + 1) * 384], gq[k]) for k in range(3)))

    def input_units(part):
        which, cols = ((3, slice(0, 768)), (5, slice(768, 1536)))[part]
        out_wait(which, bg[part])
        add_terms(1, lambda r: dot_nt(bg[part][r, :], gu[:, cols]))

    def ring_copy(which, way, step):
        target = (place.i + (1, 7)[way]) % 8
        rows = (pl.ds(0, 32), pl.ds(32, 32))[way] if step == 0 else pl.ds(0, 64)
        at, k = (which, way, step, rows), way * 4 + step
        return remote(ring_out.at[at], ring_in.at[at], zs.at[2 + which, k], zr.at[2 + which, k], {"in": target})

    def ring_step(which, step):
        for way in range(2):
            block = block_of(which, place.i + (4 - step, 4 + step)[way])
            if step == 0:
                ring_out[which, way, 0] = block[...].astype(BF16)
            else:
                ring_copy(which, way, step - 1).wait_recv()
                if step == 1:
                    half = (slice(0, 32), slice(32, 64))[way]
                    block[half, :] += ring_in[which, way, 0, half, :].astype(F32)
                    ring_out[which, way, 1] = block[...].astype(BF16)
                else:
                    ring_out[which, way, step] = (block[...] + ring_in[which, way, step - 1].astype(F32)).astype(BF16)
            start(ring_copy(which, way, step))

    def ring_total(which):
        total = block_of(which, place.i)[...]
        for way in range(2):
            ring_copy(which, way, 3).wait_recv()
            total = total + ring_in[which, way, 3].astype(F32)
        return total

    def finish_layer():
        lo_buf[...] = (tok[...].astype(F32) + ring_total(0)).astype(BF16)
        swap_start(2, lo_buf, lo_in, layer_out)

    def head_in():
        hd_out[...] = fan_total("in", place.i, 8, hz_out, hz_in, vs.at[0], vr.at[0])
        fan_send("dep", place.d, 8, hd_out, hd_in, vs.at[1], vr.at[1])

    def head_dep():
        ho_out[...] = fan_total("dep", place.d, 8, hd_out, hd_in, vs.at[1], vr.at[1])
        fan_send("out", place.o, 4, ho_out, ho_in, ss.at[2], sr.at[2])

    held = []

    def input_sums():
        input_grad = ring_total(1)
        scaled = input_grad * gain[...]
        held.append(scaled)
        first = jnp.sum(scaled, axis=1, keepdims=True)
        second = jnp.sum(scaled * normed[...], axis=1, keepdims=True)
        tot_out[...] = jnp.where(lane < 64, first, second)
        fan_send("out", place.o, 4, tot_out, tot_in, ss.at[1], sr.at[1])
        vz_out[...] = jnp.sum(input_grad * normed[...], axis=0, keepdims=True)
        fan_send("in", place.i, 8, vz_out, vz_in, vs.at[2], vr.at[2])

    def finish_tokens():
        totals = fan_total("out", place.o, 4, tot_out, tot_in, ss.at[1], sr.at[1])
        centred = held[0] - totals[:, :1] * (1.0 / 3072.0) - normed[...] * (totals[:, 64:65] * (1.0 / 3072.0))
        tg_buf[...] = (ups[...].astype(F32) + inverse[:, :1] * centred).astype(BF16)
        swap_start(3, tg_buf, tg_in, token_grad)

    def gain_in():
        vd_out[...] = fan_total("in", place.i, 8, vz_out, vz_in, vs.at[2], vr.at[2])
        fan_send("dep", place.d, 8, vd_out, vd_in, vs.at[3], vr.at[3])

    def finish():
        head_grad[...] = fan_total("out", place.o, 4, ho_out, ho_in, ss.at[2], sr.at[2])[:2]
        gain_grad[...] = fan_total("dep", place.d, 8, vd_out, vd_in, vs.at[3], vr.at[3])
        swap_end(2, lo_buf, lo_in, layer_out)
        swap_end(3, tg_buf, tg_in, token_grad)

    stage1(0)
    statistics()
    z_round(0, hid, 0)
    stage1(1)
    pass_left(0)
    pass_right(0)
    pass_pair(0)
    z_round(0, hid, 1)
    pass_right(1)
    stage3(0)
    stage1(2)
    z_round(0, hid, 2)
    z_round(1, grad, 0)
    pass_left(1)
    z_round(0, hid, 3)
    z_round(1, grad, 1)
    pass_pair(1)
    depart(0)
    reduce_near(0)
    pass_right(2)
    pass_left(2)
    pass_pair(2)
    transpose_hidden()
    z_round(1, grad, 2)
    stage3(1)
    z_round(1, grad, 3)
    stage3(2)
    remain(0)
    stage1(3)
    depart(1)
    reduce_near(1)
    reduce_far(0)
    heads()
    depart(2)
    reduce_near(2)
    pass_left(3)
    pass_right(3)
    remain(1)
    out_relay(0, kv)
    pass_pair(3)
    remain(2)
    reduce_far(1)
    attend(0)
    stage3(3)
    attend(1)
    reduce_far(2)
    activate()
    attend(2)
    attend_send()
    kv_across()
    depart(3)
    out_relay(2, act)
    reduce_near(3)
    down_product(0)
    down_product(1)
    down_product(2)
    out_relay(1, att)
    remain(3)
    keys_back()
    down_product(3)
    back_far(3)
    weight_product(1)
    before_back(0)
    mix()
    back_far(1)
    back_right(3)
    before_back(1)
    back_left(3)
    back_pair(3)
    out_relay(4, qg)
    ring_step(0, 0)
    back_right(1)
    back_left(1)
    back_pair(1)
    weight_product(0)
    ring_step(0, 1)
    out_relay(3, bg[0])
    input_heads()
    weight_product(2)
    out_relay(5, bg[1])
    input_units(0)
    input_units(1)
    ring_step(1, 0)
    back_far(0)
    weight_product(4)
    ring_step(1, 1)
    back_far(2)
    back_pair(0)
    back_pair(2)
    ring_step(0, 2)
    back4(1)
    back_right(0)
    ring_step(1, 2)
    back_far(4)
    back_left(0)
    ring_step(0, 3)
    back_pair(4)
    ring_step(1, 3)
    finish_layer()
    head_in()
    back_left(2)
    back_right(2)
    input_sums()
    head_dep()
    back_right(4)
    back4(0)
    back_left(4)
    finish_tokens()
    back4(3)
    back4(2)
    gain_in()
    back4(4)
    finish()
    for copy in pending:
        copy.wait_send()


def layer(tokens, gain, head_gain, upstream, wq, wo, wu, wd):
    shape = jax.ShapeDtypeStruct
    outs = [
        shape((64, 768), BF16), shape((64, 768), BF16), shape((1, 768), F32), shape((2, 128), F32),
        shape((3, 96, 384), F32), shape((48, 768), F32), shape((96, 1536), F32), shape((192, 768), F32),
    ]
    whole = pl.BlockSpec(memory_space=VMEM)
    far = [VMEM((128, 768), F32), VMEM((128, 384), BF16), VMEM((128, 384), F32), VMEM((128, 1536), BF16)]
    far += [VMEM((128, 768), BF16)] * 2
    full = [VMEM((3, 768, 384), BF16), VMEM((384, 768), BF16), VMEM((768, 1536), BF16), VMEM((1536, 768), BF16)]
    scratch = full + [VMEM((512, 768), BF16), VMEM((512, 768), BF16), VMEM((64, 768), F32), VMEM((64, 128), F32)]
    scratch += [VMEM((128, n), F32) for n in COLS[:3]]
    scratch += [VMEM((64, 128), F32), VMEM((3, 64, 128), F32)]
    for _ in range(3):
        scratch += [VMEM((256, n), F32) for n in COLS]
    scratch += far + far
    scratch += [VMEM((512, n), BF16) for n in (768, 384, 1536, 768, 768, 1152)]
    scratch += [VMEM((128, 384), BF16), VMEM((128, 384), BF16), VMEM((128, 768), F32), VMEM((128, 768), F32)]
    scratch += [VMEM((512, 768), F32), VMEM((2, 128, 768), F32), VMEM((128, 768), BF16), VMEM((128, 768), BF16)]
    scratch += [VMEM((64, 768), BF16)] * 2 + [VMEM((768, 512), BF16)] + [VMEM((64, 768), BF16)] * 4
    scratch += [VMEM((3, 768, 384), BF16), VMEM((384, 768), BF16), VMEM((768, 768), BF16), VMEM((1536, 768), BF16), VMEM((768, 768), BF16)]
    scratch += [VMEM((7, 3, 96, 384), BF16)] + [VMEM((7, rows, 768), BF16) for rows in BACK_ROWS[1:]]
    scratch += [VMEM((2, 2, 4, 64, 768), BF16)] * 2
    scratch += [VMEM((64, 128), F32), VMEM((3, 64, 128), F32)]
    scratch += [VMEM((1, 768), F32), VMEM((7, 1, 768), F32)] * 2
    scratch += [VMEM((8, 128), F32), VMEM((7, 8, 128), F32)] * 2
    scratch += [VMEM((8, 128), F32), VMEM((3, 8, 128), F32)]
    dma = pltpu.SemaphoreType.DMA
    scratch += [dma((4, 8)), dma((4, 8)), dma((4,)), dma((4, 8)), dma((4, 8)), dma((3, 3)), dma((3, 3))]
    scratch += [dma((4, 2)), dma((4, 2)), dma((6,)), dma((6,)), dma((6, 3)), dma((6, 3)), dma((3,)), dma((3,))]
    scratch += [dma((5, 8)), dma((5, 8)), dma((4, 7)), dma((4, 7)), dma((4,)), dma((4,))]
    return pl.pallas_call(
        layer_kernel,
        out_shape=outs,
        in_specs=[whole] * 4 + [pl.BlockSpec(memory_space=pl.ANY)] * 4,
        out_specs=[whole] * len(outs),
        scratch_shapes=scratch,
        compiler_params=pltpu.CompilerParams(collective_id=1, has_side_effects=True, vmem_limit_bytes=62 * 2**20),
        cost_estimate=pl.CostEstimate(flops=11 * 10**9, bytes_accessed=10**7, transcendentals=10**6),
    )(tokens, gain, head_gain, upstream, wq, wo, wu, wd)


def settle_kernel(*refs):
    sources, targets, stages, sems = refs[:8], refs[8:16], refs[16:24], refs[24]
    loads = [pltpu.make_async_copy(a, b, sems.at[0, k]) for k, (a, b) in enumerate(zip(sources, stages))]
    stores = [pltpu.make_async_copy(a, b, sems.at[1, k]) for k, (a, b) in enumerate(zip(stages, targets))]
    for copy in loads:
        copy.start()
    for load, store in zip(loads, stores):
        load.wait()
        store.start()
    for copy in stores:
        copy.wait()


def settle(*arrays):
    anywhere = pl.BlockSpec(memory_space=pl.ANY)
    return pl.pallas_call(
        settle_kernel,
        out_shape=[jax.ShapeDtypeStruct(a.shape, a.dtype) for a in arrays],
        in_specs=[anywhere] * 8,
        out_specs=[anywhere] * 8,
        scratch_shapes=[VMEM(a.shape, a.dtype) for a in arrays] + [pltpu.SemaphoreType.DMA((2, 8))],
        compiler_params=pltpu.CompilerParams(vmem_limit_bytes=60 * 2**20),
        cost_estimate=pl.CostEstimate(flops=0, bytes_accessed=8 * 10**6, transcendentals=0),
    )(*arrays)


def body(tokens, norm_gain, qkv_weight, head_gain, out_weight, up_weight, down_weight, upstream):
    layer_out, token_grad, gain_grad, head_grad, dq, do, du, dd = settle(*layer(
        tokens[0], norm_gain[None], head_gain, upstream[0],
        jnp.transpose(qkv_weight, (1, 0, 2)), out_weight, up_weight, down_weight,
    ))
    return (
        layer_out[None], token_grad[None], gain_grad[0], head_grad,
        jnp.transpose(dq, (1, 0, 2)), do, du, dd,
    )


def solution(mesh):
    placed = (
        P("dep", "in", "out"),
        P("out"),
        P(("out", "dep"), None, "in"),
        P(),
        P(("in", "dep"), "out"),
        P(("out", "dep"), "in"),
        P(("in", "dep"), "out"),
        P("dep", "in", "out"),
    )
    return jax.shard_map(
        body,
        mesh=mesh,
        in_specs=placed,
        out_specs=(
            P("dep", "in", "out"),
            P("dep", "in", "out"),
            P("out"),
            P(),
            P(("out", "dep"), None, "in"),
            P(("in", "dep"), "out"),
            P(("out", "dep"), "in"),
            P(("in", "dep"), "out"),
        ),
        check_vma=False,
    )
```

```python
import math

import jax
import jax.numpy as jnp
from jax import lax
from jax.experimental import pallas as pl
from jax.experimental.pallas import tpu as pltpu
from jax.sharding import PartitionSpec as P

MESH = pl.DeviceIdType.MESH
EPSILON = 1e-06
ROOT_HALF = 1.0 / math.sqrt(2.0)
ROOT_TWO_PI = math.sqrt(2.0 * math.pi)
SCALE = 128.0 ** (-0.5)
F32 = jnp.float32
BF16 = jnp.bfloat16
VMEM = pltpu.VMEM

TILES = (384, 384, 512, 512)
COLS = (1152, 384, 1536, 1536)
SHARD = ((96, 1152), (48, 768), (96, 1536), (192, 768))
SPLIT = (48, 32, 48, 96)
BACK_ROWS = (96, 48, 96, 192, 96)
BACK_SPLIT = (48, 32, 48, 96, 48)
RING = (1, 7, 2, 6, 3, 5, 4)


def remote(src, dst, send, recv, device):
    return pltpu.make_async_remote_copy(
        src_ref=src, dst_ref=dst, send_sem=send, recv_sem=recv, device_id=device, device_id_type=MESH
    )


class Place:
    def __init__(self):
        self.i = lax.axis_index("in")
        self.o = lax.axis_index("out")
        self.d = lax.axis_index("dep")
        d = self.d
        x, y = d // 2, d % 2
        right, left, far = (x + 1) % 4, (x + 3) % 4, (x + 2) % 4
        self.me = d
        self.r, self.l, self.f = right * 2 + y, left * 2 + y, far * 2 + y
        self.p = x * 2 + 1 - y
        self.rp, self.lp, self.fp = right * 2 + 1 - y, left * 2 + 1 - y, far * 2 + 1 - y
        self.h, self.c = self.o // 2, self.o % 2
        self.mate = self.h * 2 + 1 - self.c
        self.cross = (1 - self.h) * 2 + self.c
        self.mate_at = {"out": self.mate}
        self.cross_at = {"out": self.cross, "dep": self.p}
        self.diag_at = {"out": (1 - self.h) * 2 + 1 - self.c, "dep": self.p}
        self.diag = (1 - self.h) * 2 + 1 - self.c
        self.table = (
            (self.r, self.l, self.me, self.l, "all"),
            (self.l, self.r, self.me, self.r, "all"),
            (self.p, self.p, self.me, self.p, "all"),
            (self.r, self.l, self.l, self.f, "low"),
            (self.l, self.r, self.r, self.f, "high"),
            (self.r, self.l, self.p, self.lp, "all"),
            (self.l, self.r, self.p, self.rp, "all"),
            (self.p, self.p, self.f, self.fp, "all"),
        )


def rows_of(slot, rows, split, part):
    start = slot * rows
    if part == "all":
        return pl.ds(pl.multiple_of(start, 16), rows)
    if part == "low":
        return pl.ds(pl.multiple_of(start, 16), split)
    return pl.ds(pl.multiple_of(start + split, 16), rows - split)


def greet(place):
    barrier = pltpu.get_barrier_semaphore()
    for k in range(1, 8):
        pl.semaphore_signal(barrier, inc=1, device_id={"in": (place.i + k) % 8}, device_id_type=MESH)
        pl.semaphore_signal(barrier, inc=1, device_id={"dep": (place.d + k) % 8}, device_id_type=MESH)
    for peer in (place.mate_at, place.cross_at, place.diag_at):
        pl.semaphore_signal(barrier, inc=1, device_id=peer, device_id_type=MESH)
    pl.semaphore_wait(barrier, 17)


def dot(a, b):
    return lax.dot_general(a, b, (((1,), (0,)), ((), ())), preferred_element_type=F32)


def dot_nt(a, b):
    return lax.dot_general(a, b, (((1,), (1,)), ((), ())), preferred_element_type=F32)


def dot_tn(a, b):
    return lax.dot_general(a, b, (((0,), (0,)), ((), ())), preferred_element_type=F32)


def normalize(values):
    average = jnp.mean(values, axis=-1, keepdims=True)
    spread = jnp.mean(values * values, axis=-1, keepdims=True) - average * average
    inverse = lax.rsqrt(spread + EPSILON)
    return ((values - average) * inverse, inverse)


def normalize_back(incoming, normed, inverse):
    first = jnp.mean(incoming, axis=-1, keepdims=True)
    second = jnp.mean(incoming * normed, axis=-1, keepdims=True)
    return inverse * (incoming - first - normed * second)


def layer_kernel(
    tokens, gain, head_gain, upstream, wq, wo, wu, wd,
    layer_out, token_grad, gain_grad, head_grad, dq, do, du, dd,
    gq, go, gu, gd, hid, grad, normed, inverse, fq, fo, fu,
    stat_out, stat_in, away0, away1, away2, away3, home0, home1, home2, home3, in0, in1, in2, in3,
    xs_f, xs_q, xs_o, xs_u, xs_d, xs_e, xr_f, xr_q, xr_o, xr_u, xr_d, xr_e,
    kv, att, act, bg0, bg1, qg, qlow, alow, hats, invs, kvpart, kvin, kvs, kvr,
    tok, ups, hid_t, lo_buf, lo_in, tg_buf, tg_in,
    pq, po, pu, pd, pv, rq, ro, ru, rd, rv, ring_out, ring_in,
    tot_out, tot_in, vz_out, vz_in, vd_out, vd_in, hz_out, hz_in, hd_out, hd_in, ho_out, ho_in,
    gs, gr, gl, zs, zr, ss, sr, ms, mr, cs, cr, bs, br, ks, kr, ws, wr, vs, vr, es, er,
):
    place = Place()
    bg = (bg0, bg1)
    shards = (wq, wo, wu, wd)
    gathered = (gq, go, gu, gd)
    away, home, arrived, final = (away0, away1, away2, away3), (home0, home1, home2, home3), (in0, in1, in2, in3), (fq, fo, fu)
    partial, returned = (pq, po, pu, pd, pv), (rq, ro, ru, rd, rv)
    result = (dq, do, du.at[:, :768], dd, du.at[:, 768:])
    greet(place)
    pending = []

    def start(copy):
        copy.start()
        pending.append(copy)

    def local(src, dst, sem):
        copy = pltpu.make_async_copy(src, dst, sem)
        copy.start()
        return copy

    def slots(a, ref, rows):
        return ref.at[:, rows] if a == 0 else ref.at[rows]

    def gather_copy(a, k, receive=False):
        rows, _ = SHARD[a]
        target, _, mine, theirs, part = place.table[k]
        ref = slots(a, gathered[a], rows_of(theirs if receive else mine, rows, SPLIT[a], part))
        source = ref if receive or k > 2 else shards[a]
        return remote(source, ref, gs.at[a, k], gr.at[a, k], {"dep": target})

    def g_send(a, *kinds):
        for k in kinds:
            start(gather_copy(a, k))

    def g_wait(a, *kinds):
        for k in kinds:
            gather_copy(a, k, True).wait_recv()

    own_copies = [None] * 4

    def stage1(a):
        g_send(a, 0, 1, 2)
        rows, _ = SHARD[a]
        own_copies[a] = local(shards[a], slots(a, gathered[a], rows_of(place.me, rows, 0, "all")), gl.at[a])

    def pass_left(a):
        g_wait(a, 0)
        g_send(a, 3)

    def pass_right(a):
        g_wait(a, 1)
        g_send(a, 4)

    def pass_pair(a):
        g_wait(a, 2)
        g_send(a, 5, 6)

    def stage3(a):
        g_wait(a, 3, 4)
        g_send(a, 7)

    def stage4(a):
        g_wait(a, 5, 6, 7)
        own_copies[a].wait()

    def z_slot(ref, index):
        return ref.at[pl.ds(pl.multiple_of(index * 64, 64), 64)]

    def z_ring_copy(which, kind, ref, receive=False):
        turn = kind % 4
        if kind < 4:
            target, slot = (place.i + 1) % 8, (place.i + (7 if receive else 8) - turn) % 8
        else:
            target, slot = (place.i + 7) % 8, (place.i + (1 if receive else 0) + turn) % 8
        first = 32 if kind == 7 else 0
        at = ref.at[pl.ds(pl.multiple_of(slot * 64 + first, 32), 32 if turn == 3 else 64)]
        return remote(at, at, zs.at[which, kind], zr.at[which, kind], {"in": target})

    def z_round(which, ref, turn):
        for way in (0, 4):
            if turn > 0:
                z_ring_copy(which, way + turn - 1, ref, True).wait_recv()
            start(z_ring_copy(which, way + turn, ref))

    complete = set()

    def z_done(which, ref):
        if ("z", which) not in complete:
            complete.add(("z", which))
            for way in (0, 4):
                z_ring_copy(which, way + 3, ref, True).wait_recv()

    def fan_copy(axis, index, size, k, send, recv, sem_s, sem_r):
        if axis == "out":
            peer = (place.mate_at, place.cross_at, place.diag_at)[k - 1]
        else:
            peer = {axis: (index + k) % size}
        return remote(send, recv.at[k - 1], sem_s.at[k - 1], sem_r.at[k - 1], peer)

    def fan_send(axis, index, size, send, recv, sem_s, sem_r):
        for k in range(1, size):
            start(fan_copy(axis, index, size, k, send, recv, sem_s, sem_r))

    def fan_total(axis, index, size, send, recv, sem_s, sem_r):
        total = send[...]
        for k in range(1, size):
            fan_copy(axis, index, size, k, send, recv, sem_s, sem_r).wait_recv()
            total = total + recv[k - 1]
        return total

    def out_rows(ref, index):
        return ref.at[pl.ds(pl.multiple_of(index * 128, 128), 128)]

    def out_copy(which, k, ref, receive=False):
        sent = (place.o, place.o, place.cross)[k]
        got = (place.mate, place.cross, place.diag)[k]
        target = (place.mate_at, place.cross_at, place.mate_at)[k]
        rows = out_rows(ref, got if receive else sent)
        return remote(rows, rows, bs.at[which, k], br.at[which, k], target)

    def out_send(which, ref):
        start(out_copy(which, 1, ref))
        start(out_copy(which, 0, ref))

    def out_relay(which, ref):
        out_copy(which, 1, ref, True).wait_recv()
        start(out_copy(which, 2, ref))

    def out_wait(which, ref):
        if ("out", which) not in complete:
            complete.add(("out", which))
            out_copy(which, 0, ref, True).wait_recv()
            out_copy(which, 2, ref, True).wait_recv()

    def swap_copy(k, source, landing):
        return remote(source, landing, es.at[k], er.at[k], {"dep": place.p})

    def swap_start(k, source, landing, result):
        @pl.when(place.h == 1)
        def _():
            swap_copy(k, source, landing).start()

        @pl.when(place.h == 0)
        def _():
            result[...] = source[...]

    def swap_end(k, source, landing, result):
        @pl.when(place.h == 1)
        def _():
            swap_copy(k, source, landing).wait()
            if result is not landing:
                result[...] = landing[...]

    swap_start(0, tokens, tok, tok)
    swap_start(1, upstream, ups, ups)
    lane = lax.broadcasted_iota(jnp.int32, (64, 128), 1)

    def statistics():
        swap_end(0, tokens, tok, tok)
        wide = tok[...].astype(F32)
        total = jnp.sum(wide, axis=1, keepdims=True)
        square = jnp.sum(wide * wide, axis=1, keepdims=True)
        stat_out[...] = jnp.where(lane < 64, total, square)
        fan_send("out", place.o, 4, stat_out, stat_in, ss.at[0], sr.at[0])
        swap_end(1, upstream, ups, ups)
        z_slot(grad, place.i)[...] = ups[...]
        stats = fan_total("out", place.o, 4, stat_out, stat_in, ss.at[0], sr.at[0])
        average = stats[:, :1] * (1.0 / 3072.0)
        spread = stats[:, 64:65] * (1.0 / 3072.0) - average * average
        inv = lax.rsqrt(spread + EPSILON)
        norm = (wide - average) * inv
        normed[...] = norm
        inverse[...] = jnp.broadcast_to(inv, (64, 128))
        z_slot(hid, place.i)[...] = (norm * gain[...].reshape(1, 768)).astype(BF16)

    def product(a, half, out):
        left = (hid if a in (0, 2) else grad)[pl.ds(pl.multiple_of(half * 256, 256), 256), :]
        tile = TILES[a]

        @pl.loop(0, COLS[a] // tile)
        def _(t):
            cols = pl.ds(pl.multiple_of(t * tile, 128), tile)
            if a == 0:
                out[:, cols] = dot(left, gathered[a][t])
            elif a == 2:
                out[:, cols] = dot(left, gathered[a][:, cols])
            else:
                out[:, cols] = dot_nt(left, gathered[a][cols, :])

    theirs = pl.ds(pl.multiple_of((1 - place.c) * 128, 128), 128)
    ours = pl.ds(pl.multiple_of(place.c * 128, 128), 128)

    def mate_copy(a, k):
        return remote(
            (away, home)[k][a].at[theirs], arrived[a].at[pl.ds(k * 128, 128)], ms.at[a, k], mr.at[a, k], place.mate_at
        )

    far_parts = (
        ((xs_f, xr_f, 0, 0, 768), (xs_q, xr_q, 1, 768, 384)),
        ((xs_o, xr_o, 2, 0, 384),),
        ((xs_u, xr_u, 3, 0, 1536),),
        ((xs_d, xr_d, 4, 0, 768), (xs_e, xr_e, 5, 768, 768)),
    )

    def cross_copy(send, recv, k):
        return remote(send, recv, cs.at[k], cr.at[k], place.cross_at)

    def depart(a):
        stage4(a)
        z_done(*((0, hid) if a in (0, 2) else (1, grad)))
        product(a, 1 - place.h, away[a])
        mate_copy(a, 0).start()

    def remain(a):
        product(a, place.h, home[a])
        mate_copy(a, 1).start()

    def reduce_near(a):
        mate_copy(a, 0).wait_recv()
        for send, recv, k, first, count in far_parts[a]:
            cols = slice(first, first + count)
            send[...] = (away[a][ours, cols] + arrived[a][:128, cols]).astype(send.dtype)
            start(cross_copy(send, recv, k))

    def home_wait(a):
        if ("home", a) not in complete:
            complete.add(("home", a))
            mate_copy(a, 1).wait_recv()
            for k in range(2):
                mate_copy(a, k).wait_send()

    def far_sum(a, part):
        send, recv, k, first, count = far_parts[a][part]
        cols = slice(first, first + count)
        cross_copy(send, recv, k).wait_recv()
        return cols, home[a][ours, cols] + arrived[a][128:, cols] + recv[...].astype(F32)

    def reduce_far(a):
        home_wait(a)
        for part in range(len(far_parts[a])):
            cols, total = far_sum(a, part)
            final[a][:, cols] = total

    def transpose_hidden():
        z_done(0, hid)
        hid_t[...] = hid[...].T

    mine = pl.ds(pl.multiple_of(place.o * 128, 128), 128)

    def heads():
        for j in range(3):
            cols = slice(j * 128, (j + 1) * 128)
            for part in range(2):
                at = slice(part * 384 + j * 128, part * 384 + (j + 1) * 128)
                hat, hat_inv = normalize(fq[:, at])
                hats[:, at] = hat
                invs[:, at] = jnp.broadcast_to(hat_inv, (128, 128))
                low = (hat * head_gain[part : part + 1, :]).astype(BF16)
                if part == 0:
                    qlow[:, cols] = low
                else:
                    kv[mine, cols] = low
        kv[mine, 384:768] = fq[:, 768:1152].astype(BF16)
        out_send(0, kv)

    gains = []

    def attend(j):
        if j == 0:
            out_wait(0, kv)
            alow[...] = fo[...].astype(BF16)
        cols = slice(j * 128, (j + 1) * 128)
        vals = slice(384 + j * 128, 384 + (j + 1) * 128)
        query, incoming = qlow[:, cols], alow[:, cols]
        keys, values = kv[:, cols], kv[:, vals]
        scores = dot_nt(query, keys) * SCALE
        raised = jnp.exp(scores - jnp.max(scores, axis=-1, keepdims=True))
        weights = raised / jnp.sum(raised, axis=-1, keepdims=True)
        weights_low = weights.astype(BF16)
        att[mine, cols] = dot(weights_low, values).astype(BF16)
        slopes = dot_nt(incoming, values)
        centre = jnp.sum(weights * slopes, axis=-1, keepdims=True)
        score_grad = (weights * (slopes - centre)).astype(BF16)
        kvpart[:, cols] = dot_tn(score_grad, query) * SCALE
        kvpart[:, vals] = dot_tn(weights_low, incoming)
        query_grad = dot(score_grad, keys) * SCALE
        hat = hats[:, cols]
        gain_part = jnp.sum(query_grad * hat, axis=0, keepdims=True)
        back = normalize_back(query_grad * head_gain[0:1, :], hat, invs[:, cols])
        qg[mine, cols] = back.astype(BF16)
        gains.append(gain_part)

    def kv_near(h):
        rows = pl.ds(pl.multiple_of(h * 256 + (1 - place.c) * 128, 128), 128)
        return remote(kvpart.at[rows], kvin.at[h], ks.at[h], kr.at[h], place.mate_at)

    kv_far = remote(kvs, kvr, ks.at[2], kr.at[2], place.cross_at)
    def before_tile(t):
        cols = pl.ds(pl.multiple_of(t * 512, 512), 512)
        before = fu[:, cols]
        return cols, before, 0.5 * (1.0 + lax.erf(before * ROOT_HALF))

    def attend_send():
        for h in range(2):
            start(kv_near(h))
        out_send(1, att)

    def kv_across():
        for h in range(2):
            kv_near(h).wait_recv()
        other = pl.ds(pl.multiple_of(place.cross * 128, 128), 128)
        kvs[...] = (kvpart[other, :] + kvin[1 - place.h]).astype(kvs.dtype)
        start(kv_far)

    def activate():
        @pl.loop(0, 3)
        def _(t):
            cols, before, below = before_tile(t)
            act[mine, cols] = (before * below).astype(BF16)
            fu[:, cols] = below + before * jnp.exp(-0.5 * before * before) / ROOT_TWO_PI

        out_send(2, act)

    def before_back(part):
        home_wait(3)
        cols, total = far_sum(3, part)
        bg[part][mine, :] = (total * fu[:, cols]).astype(BF16)
        out_send((3, 5)[part], bg[part])

    def keys_back():
        kv_far.wait_recv()
        key_gain = jnp.zeros((1, 128), F32)
        for j in range(3):
            cols = slice(j * 128, (j + 1) * 128)
            keys = slice(384 + j * 128, 384 + (j + 1) * 128)
            vals = slice(768 + j * 128, 768 + (j + 1) * 128)
            key_grad = kvpart[mine, cols] + kvin[place.h, :, cols] + kvr[:, cols].astype(F32)
            hat = hats[:, keys]
            key_gain = key_gain + jnp.sum(key_grad * hat, axis=0, keepdims=True)
            back = normalize_back(key_grad * head_gain[1:2, :], hat, invs[:, keys])
            qg[mine, keys] = back.astype(BF16)
            value_grad = kvpart[mine, keys] + kvin[place.h, :, keys] + kvr[:, keys].astype(F32)
            qg[mine, vals] = value_grad.astype(BF16)
        out_send(4, qg)
        row = lax.broadcasted_iota(jnp.int32, (8, 128), 0)
        query_gain = gains[0] + gains[1] + gains[2]
        hz_out[...] = jnp.where(row == 0, query_gain, jnp.where(row == 1, key_gain, 0.0))
        fan_send("in", place.i, 8, hz_out, hz_in, vs.at[0], vr.at[0])

    def down_product(turn):
        if turn == 0:
            out_wait(2, act)
            z_done(1, grad)
        slot = (place.f, place.l, place.r, place.me)[turn]
        cols = pl.ds(pl.multiple_of((slot // 2) * 384, 128), 384)
        pd[cols, :] = dot_tn(act[:, cols], grad[...]).astype(BF16)
        if turn < 3:
            b_send(3, (7, 5, 6)[turn])

    def weight_product(a):
        if a == 0:
            out_wait(4, qg)

            @pl.loop(0, 3)
            def _(t):
                pq[t] = dot(hid_t[...], qg[:, pl.ds(pl.multiple_of(t * 384, 128), 384)]).astype(BF16)
        elif a == 1:
            out_wait(1, att)
            po[...] = dot_tn(att[...], grad[...]).astype(BF16)
        else:
            which, right, target = (3, bg[0], pu) if a == 2 else (5, bg[1], pv)
            out_wait(which, right)

            @pl.loop(0, 2)
            def _(t):
                cols = pl.ds(pl.multiple_of(t * 384, 128), 384)
                target[:, cols] = dot(hid_t[...], right[:, cols]).astype(BF16)

        b_send(a, 7, 5, 6)

    def back_place(a, k):
        rows = BACK_ROWS[a]
        part = place.table[k][4]
        slot = (0, 1, 2, 3, 3, 4, 5, 6)[k]
        if part == "all":
            return returned[a].at[slot]
        if part == "low":
            return slots(a, returned[a].at[slot], pl.ds(0, BACK_SPLIT[a]))
        return slots(a, returned[a].at[slot], pl.ds(BACK_SPLIT[a], rows - BACK_SPLIT[a]))

    def back_copy(a, k):
        rows = BACK_ROWS[a]
        _, target, _, slot, part = place.table[k]
        source = slots(a, partial[a], rows_of(slot, rows, BACK_SPLIT[a], part))
        return remote(source, back_place(a, k), ws.at[a, k], wr.at[a, k], {"dep": target})

    def b_send(a, *kinds):
        for k in kinds:
            start(back_copy(a, k))

    def b_add(a, *kinds):
        rows = BACK_ROWS[a]
        for k in kinds:
            back_copy(a, k).wait_recv()
        _, _, slot, _, part = place.table[kinds[0]]
        at = slots(a, partial[a], rows_of(slot, rows, BACK_SPLIT[a], part))
        total = at[...].astype(F32)
        for k in kinds:
            total = total + back_place(a, k)[...].astype(F32)
        return at, total

    def b_merge(a, *kinds):
        at, total = b_add(a, *kinds)
        at[...] = total.astype(BF16)

    def back_far(a):
        b_merge(a, 7)
        b_send(a, 3, 4)

    def back_pair(a):
        b_merge(a, 5, 6)
        b_send(a, 2)

    def back_left(a):
        b_merge(a, 3)
        b_send(a, 0)

    def back_right(a):
        b_merge(a, 4)
        b_send(a, 1)

    def back4(a):
        _, total = b_add(a, 0, 1, 2)
        result[a][...] = total

    totals_of = (home2, away2)

    def block_of(which, index):
        index = index % 8
        rows = pl.ds(pl.multiple_of((index % 4) * 64, 64), 64)
        return totals_of[which].at[rows, pl.ds(pl.multiple_of((index // 4) * 768, 128), 768)]

    def add_terms(which, term):
        for b in range(2):
            rows, cols = slice(b * 256, (b + 1) * 256), slice(b * 768, (b + 1) * 768)
            value = term(rows)
            if which in complete:
                value = totals_of[which][:, cols] + value
            totals_of[which][:, cols] = value
        complete.add(which)

    def mix():
        out_wait(1, att)
        out_wait(2, act)
        add_terms(0, lambda r: dot(att[r, :], go[...]) + dot(act[r, :], gd[...]))

    def input_heads():
        out_wait(4, qg)
        add_terms(1, lambda r: sum(dot_nt(qg[r, k * 384 : (k + 1) * 384], gq[k]) for k in range(3)))

    def input_units(part):
        which, cols = ((3, slice(0, 768)), (5, slice(768, 1536)))[part]
        out_wait(which, bg[part])
        add_terms(1, lambda r: dot_nt(bg[part][r, :], gu[:, cols]))

    def ring_copy(which, way, step):
        target = (place.i + (1, 7)[way]) % 8
        rows = (pl.ds(0, 32), pl.ds(32, 32))[way] if step == 0 else pl.ds(0, 64)
        at, k = (which, way, step, rows), way * 4 + step
        return remote(ring_out.at[at], ring_in.at[at], zs.at[2 + which, k], zr.at[2 + which, k], {"in": target})

    def ring_step(which, step):
        for way in range(2):
            block = block_of(which, place.i + (4 - step, 4 + step)[way])
            if step == 0:
                ring_out[which, way, 0] = block[...].astype(BF16)
            else:
                ring_copy(which, way, step - 1).wait_recv()
                if step == 1:
                    half = (slice(0, 32), slice(32, 64))[way]
                    block[half, :] += ring_in[which, way, 0, half, :].astype(F32)
                    ring_out[which, way, 1] = block[...].astype(BF16)
                else:
                    ring_out[which, way, step] = (block[...] + ring_in[which, way, step - 1].astype(F32)).astype(BF16)
            start(ring_copy(which, way, step))

    def ring_total(which):
        total = block_of(which, place.i)[...]
        for way in range(2):
            ring_copy(which, way, 3).wait_recv()
            total = total + ring_in[which, way, 3].astype(F32)
        return total

    def finish_layer():
        lo_buf[...] = (tok[...].astype(F32) + ring_total(0)).astype(BF16)
        swap_start(2, lo_buf, lo_in, layer_out)

    def head_in():
        hd_out[...] = fan_total("in", place.i, 8, hz_out, hz_in, vs.at[0], vr.at[0])
        fan_send("dep", place.d, 8, hd_out, hd_in, vs.at[1], vr.at[1])

    def head_dep():
        ho_out[...] = fan_total("dep", place.d, 8, hd_out, hd_in, vs.at[1], vr.at[1])
        fan_send("out", place.o, 4, ho_out, ho_in, ss.at[2], sr.at[2])

    held = []

    def input_sums():
        input_grad = ring_total(1)
        scaled = input_grad * gain[...].reshape(1, 768)
        held.append(scaled)
        first = jnp.sum(scaled, axis=1, keepdims=True)
        second = jnp.sum(scaled * normed[...], axis=1, keepdims=True)
        tot_out[...] = jnp.where(lane < 64, first, second)
        fan_send("out", place.o, 4, tot_out, tot_in, ss.at[1], sr.at[1])
        vz_out[...] = jnp.sum(input_grad * normed[...], axis=0, keepdims=True)
        fan_send("in", place.i, 8, vz_out, vz_in, vs.at[2], vr.at[2])

    def finish_tokens():
        totals = fan_total("out", place.o, 4, tot_out, tot_in, ss.at[1], sr.at[1])
        centred = held[0] - totals[:, :1] * (1.0 / 3072.0) - normed[...] * (totals[:, 64:65] * (1.0 / 3072.0))
        tg_buf[...] = (ups[...].astype(F32) + inverse[:, :1] * centred).astype(BF16)
        swap_start(3, tg_buf, tg_in, token_grad)

    def gain_in():
        vd_out[...] = fan_total("in", place.i, 8, vz_out, vz_in, vs.at[2], vr.at[2])
        fan_send("dep", place.d, 8, vd_out, vd_in, vs.at[3], vr.at[3])

    def finish():
        head_grad[...] = fan_total("out", place.o, 4, ho_out, ho_in, ss.at[2], sr.at[2])[:2]
        gain_grad[...] = fan_total("dep", place.d, 8, vd_out, vd_in, vs.at[3], vr.at[3]).reshape(768)
        swap_end(2, lo_buf, lo_in, layer_out)
        swap_end(3, tg_buf, tg_in, token_grad)

    stage1(0)
    statistics()
    z_round(0, hid, 0)
    stage1(1)
    pass_left(0)
    pass_right(0)
    pass_pair(0)
    z_round(0, hid, 1)
    pass_right(1)
    stage3(0)
    stage1(2)
    z_round(0, hid, 2)
    z_round(1, grad, 0)
    pass_left(1)
    z_round(0, hid, 3)
    z_round(1, grad, 1)
    pass_pair(1)
    depart(0)
    reduce_near(0)
    pass_right(2)
    pass_left(2)
    pass_pair(2)
    transpose_hidden()
    z_round(1, grad, 2)
    stage3(1)
    z_round(1, grad, 3)
    stage3(2)
    remain(0)
    stage1(3)
    depart(1)
    reduce_near(1)
    reduce_far(0)
    heads()
    depart(2)
    reduce_near(2)
    pass_left(3)
    pass_right(3)
    remain(1)
    out_relay(0, kv)
    pass_pair(3)
    remain(2)
    reduce_far(1)
    attend(0)
    stage3(3)
    attend(1)
    reduce_far(2)
    activate()
    attend(2)
    attend_send()
    kv_across()
    depart(3)
    out_relay(2, act)
    reduce_near(3)
    down_product(0)
    down_product(1)
    down_product(2)
    out_relay(1, att)
    remain(3)
    keys_back()
    down_product(3)
    back_far(3)
    weight_product(1)
    before_back(0)
    mix()
    back_far(1)
    back_right(3)
    before_back(1)
    back_left(3)
    back_pair(3)
    out_relay(4, qg)
    ring_step(0, 0)
    back_right(1)
    back_left(1)
    back_pair(1)
    weight_product(0)
    ring_step(0, 1)
    out_relay(3, bg[0])
    input_heads()
    weight_product(2)
    out_relay(5, bg[1])
    input_units(0)
    input_units(1)
    ring_step(1, 0)
    back_far(0)
    weight_product(4)
    ring_step(1, 1)
    back_far(2)
    back_pair(0)
    back_pair(2)
    ring_step(0, 2)
    back4(1)
    back_right(0)
    ring_step(1, 2)
    back_far(4)
    back_left(0)
    ring_step(0, 3)
    back_pair(4)
    ring_step(1, 3)
    finish_layer()
    head_in()
    back_left(2)
    back_right(2)
    input_sums()
    head_dep()
    back_right(4)
    back4(0)
    back_left(4)
    finish_tokens()
    back4(3)
    back4(2)
    gain_in()
    back4(4)
    finish()
    for copy in pending:
        copy.wait_send()


def layer(tokens, gain, head_gain, upstream, wq, wo, wu, wd):
    shape = jax.ShapeDtypeStruct
    outs = [
        shape((64, 768), BF16), shape((64, 768), BF16), shape((768,), F32), shape((2, 128), F32),
        shape((3, 96, 384), F32), shape((48, 768), F32), shape((96, 1536), F32), shape((192, 768), F32),
    ]
    whole = pl.BlockSpec(memory_space=VMEM)
    far = [VMEM((128, 768), F32), VMEM((128, 384), BF16), VMEM((128, 384), F32), VMEM((128, 1536), BF16)]
    far += [VMEM((128, 768), BF16)] * 2
    full = [VMEM((3, 768, 384), BF16), VMEM((384, 768), BF16), VMEM((768, 1536), BF16), VMEM((1536, 768), BF16)]
    scratch = full + [VMEM((512, 768), BF16), VMEM((512, 768), BF16), VMEM((64, 768), F32), VMEM((64, 128), F32)]
    scratch += [VMEM((128, n), F32) for n in COLS[:3]]
    scratch += [VMEM((64, 128), F32), VMEM((3, 64, 128), F32)]
    for _ in range(3):
        scratch += [VMEM((256, n), F32) for n in COLS]
    scratch += far + far
    scratch += [VMEM((512, n), BF16) for n in (768, 384, 1536, 768, 768, 1152)]
    scratch += [VMEM((128, 384), BF16), VMEM((128, 384), BF16), VMEM((128, 768), F32), VMEM((128, 768), F32)]
    scratch += [VMEM((512, 768), F32), VMEM((2, 128, 768), F32), VMEM((128, 768), BF16), VMEM((128, 768), BF16)]
    scratch += [VMEM((64, 768), BF16)] * 2 + [VMEM((768, 512), BF16)] + [VMEM((64, 768), BF16)] * 4
    scratch += [VMEM((3, 768, 384), BF16), VMEM((384, 768), BF16), VMEM((768, 768), BF16), VMEM((1536, 768), BF16), VMEM((768, 768), BF16)]
    scratch += [VMEM((7, 3, 96, 384), BF16)] + [VMEM((7, rows, 768), BF16) for rows in BACK_ROWS[1:]]
    scratch += [VMEM((2, 2, 4, 64, 768), BF16)] * 2
    scratch += [VMEM((64, 128), F32), VMEM((3, 64, 128), F32)]
    scratch += [VMEM((1, 768), F32), VMEM((7, 1, 768), F32)] * 2
    scratch += [VMEM((8, 128), F32), VMEM((7, 8, 128), F32)] * 2
    scratch += [VMEM((8, 128), F32), VMEM((3, 8, 128), F32)]
    dma = pltpu.SemaphoreType.DMA
    scratch += [dma((4, 8)), dma((4, 8)), dma((4,)), dma((4, 8)), dma((4, 8)), dma((3, 3)), dma((3, 3))]
    scratch += [dma((4, 2)), dma((4, 2)), dma((6,)), dma((6,)), dma((6, 3)), dma((6, 3)), dma((3,)), dma((3,))]
    scratch += [dma((5, 8)), dma((5, 8)), dma((4, 7)), dma((4, 7)), dma((4,)), dma((4,))]
    return pl.pallas_call(
        layer_kernel,
        out_shape=outs,
        in_specs=[whole] * 4 + [pl.BlockSpec(memory_space=pl.ANY)] * 4,
        out_specs=[whole] * len(outs),
        scratch_shapes=scratch,
        compiler_params=pltpu.CompilerParams(collective_id=1, has_side_effects=True, vmem_limit_bytes=62 * 2**20),
        cost_estimate=pl.CostEstimate(flops=11 * 10**9, bytes_accessed=10**7, transcendentals=10**6),
    )(tokens, gain, head_gain, upstream, wq, wo, wu, wd)


def settle_kernel(*refs):
    sources, targets, stages, sems = refs[:8], refs[8:16], refs[16:24], refs[24]
    loads = [pltpu.make_async_copy(a, b, sems.at[0, k]) for k, (a, b) in enumerate(zip(sources, stages))]
    stores = [pltpu.make_async_copy(a, b, sems.at[1, k]) for k, (a, b) in enumerate(zip(stages, targets))]
    for copy in loads:
        copy.start()
    for load, store in zip(loads, stores):
        load.wait()
        store.start()
    for copy in stores:
        copy.wait()


def settle(*arrays):
    anywhere = pl.BlockSpec(memory_space=pl.ANY)
    return pl.pallas_call(
        settle_kernel,
        out_shape=[jax.ShapeDtypeStruct(a.shape, a.dtype) for a in arrays],
        in_specs=[anywhere] * 8,
        out_specs=[anywhere] * 8,
        scratch_shapes=[VMEM(a.shape, a.dtype) for a in arrays] + [pltpu.SemaphoreType.DMA((2, 8))],
        compiler_params=pltpu.CompilerParams(vmem_limit_bytes=60 * 2**20),
        cost_estimate=pl.CostEstimate(flops=0, bytes_accessed=8 * 10**6, transcendentals=0),
    )(*arrays)


def body(tokens, norm_gain, qkv_weight, head_gain, out_weight, up_weight, down_weight, upstream):
    layer_out, token_grad, gain_grad, head_grad, dq, do, du, dd = settle(*layer(
        tokens[0], norm_gain, head_gain, upstream[0],
        jnp.transpose(qkv_weight, (1, 0, 2)), out_weight, up_weight, down_weight,
    ))
    return (
        layer_out[None], token_grad[None], gain_grad, head_grad,
        jnp.transpose(dq, (1, 0, 2)), do, du, dd,
    )


def solution(mesh):
    placed = (
        P("dep", "in", "out"),
        P("out"),
        P(("out", "dep"), None, "in"),
        P(),
        P(("in", "dep"), "out"),
        P(("out", "dep"), "in"),
        P(("in", "dep"), "out"),
        P("dep", "in", "out"),
    )
    return jax.shard_map(
        body,
        mesh=mesh,
        in_specs=placed,
        out_specs=(
            P("dep", "in", "out"),
            P("dep", "in", "out"),
            P("out"),
            P(),
            P(("out", "dep"), None, "in"),
            P(("in", "dep"), "out"),
            P(("out", "dep"), "in"),
            P(("in", "dep"), "out"),
        ),
        check_vma=False,
    )
```
